256 devices in a mesh: day: 4 (over x), sky: 64 (over y, z, core).
Axes of the slice: x: 4, y: 4, z: 8, core: 2. Of those that a mesh axis runs over, the one named last changes fastest.
Arguments:
- visibility: bfloat16 [4, 4, 4096, 2048], P('day', None, 'sky'), may hold values from -6 to 6
- flags: int32 [4, 4096, 1024], P('day', 'sky'), may hold values 0 or 1
- counts: int32 [4, 4096], P('day', 'sky'), may hold values from 1 to 9
- m_order: int32 [640], replicated, may hold values from 0 to 639, each once
- projection: bfloat16 [4, 640, 2048, 128], P('day', 'sky'), may hold values from -0.125 to 0.125
- singular: float32 [4, 640, 128], P('day', 'sky'), may hold values from 0.05 to 5
- cycles_basis: bfloat16 [4, 640, 128, 2, 1024], P('day', 'sky'), may hold values from -0.5 to 0.5
Outputs:
- sky_map: float32 [4, 1024, 2048], P('day', 'sky')
The draws below stay inside these ranges and needn't reach their ends.
Inputs may be any that keep to these rules, and one draw needn't show every extreme that they name: m_order holds every number of 0 to 639 once.
All inputs are finite; a program needn't handle non-finite values. No bound on the sum of `flags` on one device may be relied on, other than what follows from the above.
Results may differ from the reference program's by a relative error of at most 0.009.
Values may be sent and summed in bfloat16 or wider, within the bound.
No kernel may reach another device: no remote copies, remote signals or barrier semaphores. Data moves between devices by JAX's collectives and lax.ppermute only.
A program may use at most 128 MiB of HBM per device.

```python
import math
import jax
import jax.numpy as jnp
from jax import lax

NB = 1024
NT = 4096
NM = 640
NK = 128
NR = 1024
NPHI = 2048
CH = 4
N_DAY = 4


def place_ends(drawn, rng, low, high):
    dims = drawn.shape
    spot = [jax.random.randint(jax.random.fold_in(rng, axis), (), 0, dims[axis]) for axis in range(len(dims))]
    drawn = drawn.at[tuple(spot)].set(low)
    longest = dims.index(max(dims))
    spot[longest] = (spot[longest] + 1) % dims[longest]
    return drawn.at[tuple(spot)].set(high)


def block_levels(rng, extent, cuts, low, high):
    def one(dim, blocks):
        steps = jax.random.uniform(jax.random.fold_in(jax.random.fold_in(rng, 6), dim), (blocks,), jnp.float32, low / len(cuts), high / len(cuts))
        return jnp.repeat(jnp.exp(steps), extent[dim] // blocks).reshape((-1,) + (1,) * (len(extent) - dim - 1))

    loudness = one(*cuts[0])
    for cut in cuts[1:]:
        loudness = loudness * one(*cut)
    return loudness


def noise(rng, dims, deviation, most, cuts=(), kind=jnp.bfloat16):
    drawn = jax.random.normal(rng, dims, jnp.float32) * deviation
    if len(cuts) > 0:
        drawn = block_levels(rng, dims, cuts, -0.22, 0.18) * drawn
    return jnp.clip(drawn, min=-most, max=most).astype(kind)


def setup_inputs(seed: int = 0) -> dict:
    seeds = jax.random.split(jax.random.key(seed), 8)
    return {
        "visibility": noise(seeds[0], (N_DAY, CH, NT, 2 * NB), 1.0, 6.0, ((0, 4), (2, 64))),
        "flags": place_ends((jax.random.randint(seeds[1], (N_DAY, NT, NB), 0, 4) < 3).astype(jnp.int32), jax.random.fold_in(seeds[1], 1), 0, 1),
        "counts": place_ends(jax.random.randint(seeds[2], (N_DAY, NT), 1, 10), jax.random.fold_in(seeds[2], 1), 1, 9).astype(jnp.int32),
        "m_order": jax.random.permutation(seeds[3], NM).astype(jnp.int32),
        "projection": noise(seeds[4], (CH, NM, 2 * NB, NK), (2 * NB) ** -0.5, 0.125, ((0, 4), (1, 64))),
        "singular": jnp.clip(jnp.exp(math.log(5.0) - 4.6051702 * jax.random.uniform(seeds[5], (CH, NM, NK), jnp.float32) ** block_levels(seeds[5], (CH, NM, NK), ((0, 4), (1, 64)), -0.2, 0.2)), 0.05, 5.0),
        "cycles_basis": noise(seeds[6], (CH, NM, NK, 2, NR), NK ** -0.5, 0.5, ((0, 4), (1, 64))),
    }


def tables(modes, times, period):
    turns = modes[:, None] * times[None, :] % period
    angle = turns.astype(jnp.float32) * (2.0 * math.pi / period)
    return (jnp.cos(angle).astype(jnp.bfloat16), jnp.sin(angle).astype(jnp.bfloat16))

def combine(first, second):
    shape = first.shape
    first = first.reshape(shape[:-1] + (shape[-1] // 2, 2))
    second = second.reshape(shape[:-1] + (shape[-1] // 2, 2))
    real_part = first[..., 0] + second[..., 1]
    imag_part = first[..., 1] - second[..., 0]
    return jnp.stack([real_part, imag_part], axis=-1).reshape(shape)

def reference(visibility, flags, counts, m_order, projection, singular, cycles_basis):
    flag_values = flags.astype(jnp.float32)
    den = lax.optimization_barrier(jnp.sum(flag_values * counts.astype(jnp.float32)[:, :, None], axis=0))
    num = jnp.zeros((CH, NT, 2 * NB), jnp.float32)
    for group in range(visibility.shape[0]):
        pairs = jnp.repeat(flag_values[group], 2, axis=1)
        num = num + visibility[group].astype(jnp.float32) * pairs[None]
    averaged = (num / jnp.repeat(jnp.maximum(den, 1.0), 2, axis=1)[None]).astype(jnp.bfloat16)
    cosine, sine = tables(m_order, jnp.arange(NT, dtype=jnp.int32), NT)
    cosine_p, sine_p = tables(m_order, jnp.arange(NPHI, dtype=jnp.int32), NPHI)
    rank = NK - NK * m_order // (2 * NM)
    keep = jnp.arange(NK, dtype=jnp.int32)[None, :] < rank[:, None]
    maps = []
    for chan in range(CH):
        first = jnp.dot(cosine, averaged[chan], preferred_element_type=jnp.float32)
        second = jnp.dot(sine, averaged[chan], preferred_element_type=jnp.float32)
        mvis = (combine(first, second) * (1.0 / math.sqrt(NT))).astype(jnp.bfloat16)
        sing = singular[chan]
        weight = jnp.where(keep, sing / (sing * sing + 0.25), 0.0)
        raw = jnp.einsum('mb,mbk->mk', mvis.astype(jnp.float32), projection[chan].astype(jnp.float32))
        coef = (raw * weight).astype(jnp.bfloat16)
        profile = jnp.einsum('mk,mkqr->mqr', coef.astype(jnp.float32), cycles_basis[chan].astype(jnp.float32)).astype(jnp.bfloat16)
        real_sum = jnp.dot(profile[:, 0].T, cosine_p, preferred_element_type=jnp.float32)
        imag_sum = jnp.dot(profile[:, 1].T, sine_p, preferred_element_type=jnp.float32)
        maps.append((real_sum - imag_sum) / math.sqrt(NM))
    return jnp.stack(maps, axis=0)
```

```python
import math

import jax
import jax.numpy as jnp
import ml_dtypes
import numpy as np
from jax import lax
from jax.experimental import pallas as pl
from jax.experimental.pallas import tpu as pltpu
from jax.sharding import Mesh
from jax.sharding import PartitionSpec as P

NB, NT, NM, NK, NR, NPHI = 1024, 4096, 640, 128, 1024, 2048
ND, NY, NZ, NC = 4, 4, 8, 2
SKY = NY * NZ * NC
NJ = NY * NC
JW = 2 * NB // NJ
BW = NB // NJ
TL = NT // SKY
TZ = TL * NJ
OS = NM // SKY
OR = NR // SKY
CW = JW + BW
PR = 24
BF, F32 = jnp.bfloat16, jnp.float32


def transform_table():
    m = np.arange(NM)
    y, z, c, t = np.ix_(np.arange(NY), np.arange(NZ), np.arange(NC), np.arange(TL))
    times = (((y * NZ + z) * NC + c) * TL + t).transpose(1, 0, 2, 3).reshape(NZ, TZ)
    angle = (m[None, :, None] * times[:, None, :] % NT) * (2.0 * math.pi / NT)
    return np.concatenate([np.cos(angle), np.sin(angle)], axis=2).astype(ml_dtypes.bfloat16)


def synthesis_table():
    angle = (np.arange(NM)[:, None] * np.arange(NPHI)[None, :] % NPHI) * (2.0 * math.pi / NPHI)
    return np.concatenate([np.cos(angle), -np.sin(angle)], axis=0).astype(ml_dtypes.bfloat16)


def iota(shape, dim):
    return lax.broadcasted_iota(jnp.int32, shape, dim)


def spread():
    return jnp.where(iota((BW, JW), 0) == iota((BW, JW), 1) // 2, 1.0, 0.0).astype(BF)


def dot(a, b):
    return jnp.dot(a, b, preferred_element_type=F32)


def pack_kernel(vis_ref, flags_ref, counts_ref, out_ref):
    eye = iota((TL, TL), 0) == iota((TL, TL), 1)
    counts = jnp.where(eye, counts_ref[...].astype(F32), 0.0).astype(BF)
    good = flags_ref[...].astype(F32).astype(BF)
    terms = dot(counts, good).astype(BF)
    expand = spread()
    for j in range(NJ):
        mask = dot(good[:, j * BW : (j + 1) * BW], expand)
        block = vis_ref[0, :, j * JW : (j + 1) * JW].astype(F32) * mask
        out_ref[j, :, 0:JW] = block.astype(BF)
        out_ref[j, :, JW:CW] = terms[:, j * BW : (j + 1) * BW]


def pack(vis, flags, counts):
    return pl.pallas_call(
        pack_kernel,
        grid=(ND,),
        in_specs=[
            pl.BlockSpec((1, TL, 2 * NB), lambda c: (c, 0, 0)),
            pl.BlockSpec((TL, NB), lambda c: (0, 0)),
            pl.BlockSpec((1, TL), lambda c: (0, 0)),
        ],
        out_specs=pl.BlockSpec((NJ, TL, CW), lambda c: (c, 0, 0)),
        out_shape=jax.ShapeDtypeStruct((ND * NJ, TL, CW), BF),
        name="pack",
    )(vis, flags, counts)


def transform_kernel(got_ref, table_ref, order_ref, out_ref, data, swapped):
    expand = spread()
    row, col = iota((JW, JW), 0), iota((JW, JW), 1)
    swap = jnp.where(row == col + 1, jnp.where(col % 2 == 0, 1.0, 0.0), 0.0)
    swap = swap - jnp.where(col == row + 1, jnp.where(col % 2 == 1, 1.0, 0.0), 0.0)
    swap = swap.astype(BF)
    for j in range(NJ):
        num = got_ref[j, :, 0:JW].astype(F32)
        den = got_ref[j, :, JW:CW].astype(F32)
        for d in range(1, ND):
            num += got_ref[d * NJ + j, :, 0:JW].astype(F32)
            den += got_ref[d * NJ + j, :, JW:CW].astype(F32)
        den = dot(jnp.maximum(den, 1.0).astype(BF), expand)
        averaged = (num / den).astype(BF)
        data[j * TL : (j + 1) * TL, :] = averaged
        swapped[j * TL : (j + 1) * TL, :] = dot(averaged, swap).astype(BF)
    part = dot(table_ref[:, 0:TZ], data[...]) + dot(table_ref[:, TZ : 2 * TZ], swapped[...])
    part = (part * (1.0 / math.sqrt(NT))).astype(BF)
    rows = SKY * PR
    r = iota((rows, 1), 0)
    i = r % PR
    half = jnp.where(i < OS, 0, 1)
    order = order_ref[...]
    low = jnp.where(jnp.where(half == 0, order, -1) == iota((rows, NM), 1), 1.0, 0.0).astype(BF)
    high = jnp.where(jnp.where(half == 1, order, -1) == iota((rows, NM), 1), 1.0, 0.0).astype(BF)
    out_ref[...] = (dot(low, part[:, 0:NK]) + dot(high, part[:, NK : 2 * NK])).astype(BF)


def transform(got, table, packed_order):
    return pl.pallas_call(
        transform_kernel,
        out_shape=jax.ShapeDtypeStruct((SKY * PR, JW // 2), BF),
        scratch_shapes=[pltpu.VMEM((TZ, JW), BF), pltpu.VMEM((TZ, JW), BF)],
        compiler_params=pltpu.CompilerParams(vmem_limit_bytes=32 * 1024 * 1024),
        name="transform",
    )(got, table, packed_order)


def project_kernel(parts_ref, proj_ref, sing_ref, mode_ref, out_ref, mvis):
    for j in range(NJ):
        y, c = j // NC, j % NC
        total = parts_ref[(y * NZ) * NC + c].astype(F32)
        for z in range(1, NZ):
            total += parts_ref[(y * NZ + z) * NC + c].astype(F32)
        mvis[:, j * JW : j * JW + NK] = total[0:OS].astype(BF)
        mvis[:, j * JW + NK : (j + 1) * JW] = total[OS : 2 * OS].astype(BF)
    left = mvis[...]
    slot = iota((OS, NK), 0)
    raw = jnp.zeros((OS, NK), F32)
    for s in range(OS):
        raw = jnp.where(slot == s, dot(left, proj_ref[s]), raw)
    rank = NK - NK * mode_ref[...] // (2 * NM)
    sing = sing_ref[...]
    weight = jnp.where(iota((OS, NK), 1) < rank, sing / (sing * sing + 0.25), 0.0)
    out_ref[...] = (raw * weight).astype(BF)


def project(parts, projection, singular, own_modes):
    return pl.pallas_call(
        project_kernel,
        out_shape=jax.ShapeDtypeStruct((OS, NK), BF),
        scratch_shapes=[pltpu.VMEM((OS, 2 * NB), BF)],
        compiler_params=pltpu.CompilerParams(vmem_limit_bytes=32 * 1024 * 1024),
        name="project",
    )(parts, projection, singular, own_modes)


def body(visibility, flags, counts, m_order, projection, singular, cycles_basis):
    sky = ("y", "z", "core")
    sent = pack(visibility[0], flags[0], counts)
    table = lax.dynamic_index_in_dim(transform_table(), lax.axis_index("z"), 0, keepdims=False)
    slots = m_order.reshape(SKY, OS)
    none = jnp.full((SKY, PR - 2 * OS), -1, jnp.int32)
    packed_order = jnp.concatenate([slots, slots, none], axis=1).reshape(SKY * PR, 1)
    got = lax.all_to_all(sent, ("day", "y", "core"), split_axis=0, concat_axis=0, tiled=True)
    packed = transform(got, table, packed_order).reshape(SKY, PR, JW // 2)
    parts = lax.all_to_all(packed, sky, split_axis=0, concat_axis=0, tiled=True)
    own_modes = lax.dynamic_slice_in_dim(m_order, lax.axis_index(sky) * OS, OS)
    coef = project(parts, projection[0], singular[0], own_modes[:, None])
    profile = jnp.einsum("mk,mkqr->mqr", coef, cycles_basis[0], preferred_element_type=F32).astype(BF)
    gathered = lax.all_to_all(profile, sky, split_axis=2, concat_axis=0, tiled=True)
    one_hot = (m_order[:, None] == jnp.arange(NM, dtype=jnp.int32)[None, :]).astype(BF)
    natural = jnp.einsum("sqr,sm->rqm", gathered, one_hot, preferred_element_type=F32).astype(BF)
    out = dot(natural.reshape(OR, 2 * NM), synthesis_table())
    return (out * (1.0 / math.sqrt(NM)))[None]


def solution(mesh):
    fine = Mesh(mesh.devices.reshape(ND, NY, NZ, NC), ("day", "y", "z", "core"))
    sky = ("y", "z", "core")
    return jax.shard_map(
        body,
        mesh=fine,
        in_specs=(
            P("day", None, sky, None),
            P("day", sky, None),
            P("day", sky),
            P(),
            P("day", sky, None, None),
            P("day", sky, None),
            P("day", sky, None, None, None),
        ),
        out_specs=P("day", sky, None),
        check_vma=False,
    )
```

```python
import math

import jax
import jax.numpy as jnp
import ml_dtypes
import numpy as np
from jax import lax
from jax.experimental import pallas as pl
from jax.experimental.pallas import tpu as pltpu
from jax.sharding import Mesh
from jax.sharding import PartitionSpec as P

NB, NT, NM, NK, NR, NPHI = 1024, 4096, 640, 128, 1024, 2048
ND, NY, NZ, NC = 4, 4, 8, 2
SKY = NY * NZ * NC
NJ = NY * NC
JW = 2 * NB // NJ
BW = NB // NJ
TL = NT // SKY
TZ = TL * NJ
OS = NM // SKY
OR = NR // SKY
CW = JW + BW
PR = 24
QM = NM // 4
QW = 256
SP = 16
EW = 2 * SP * OR
MIB = 1024 * 1024
COST = 20_000_000
BF, F32 = jnp.bfloat16, jnp.float32


def transform_table():
    m = np.arange(NM)
    y, z, c, t = np.ix_(np.arange(NY), np.arange(NZ), np.arange(NC), np.arange(TL))
    times = (((y * NZ + z) * NC + c) * TL + t).transpose(1, 0, 2, 3).reshape(NZ, TZ)
    angle = (m[None, :, None] * times[:, None, :] % NT) * (2.0 * math.pi / NT)
    return np.concatenate([np.cos(angle), np.sin(angle)], axis=2).astype(ml_dtypes.bfloat16)


def synthesis_table():
    p = np.arange(NPHI // 4)[None, :]
    out = np.zeros((4, 2, QM, NPHI // 4))
    for r in range(4):
        angle = (np.arange(r, NM, 4)[:, None] * p % NPHI) * (2.0 * math.pi / NPHI)
        out[r, 0], out[r, 1] = np.cos(angle), -np.sin(angle)
    return out.reshape(8 * QM, NPHI // 4).astype(ml_dtypes.bfloat16)


def iota(shape, dim):
    return lax.broadcasted_iota(jnp.int32, shape, dim)


def spread():
    return jnp.where(iota((BW, JW), 0) == iota((BW, JW), 1) // 2, 1.0, 0.0).astype(BF)


def dot(a, b):
    return jnp.dot(a, b, preferred_element_type=F32)


def limit(mib):
    return pltpu.CompilerParams(vmem_limit_bytes=mib * MIB)


def stay(x):
    return pltpu.with_memory_space_constraint(x, pltpu.HBM)


def pack_kernel(vis_hbm, flags_hbm, counts_hbm, out_hbm, vis, flags, counts, masks, blocks, sems, out_sems):
    copies = [
        pltpu.make_async_copy(flags_hbm, flags, sems.at[0]),
        pltpu.make_async_copy(counts_hbm, counts, sems.at[1]),
    ] + [pltpu.make_async_copy(vis_hbm.at[c], vis.at[c], sems.at[2 + c]) for c in range(ND)]
    for copy in copies:
        copy.start()
    expand = spread()
    eye = iota((TL, TL), 0) == iota((TL, TL), 1)
    copies[0].wait()
    copies[1].wait()
    weights = jnp.where(eye, counts[...].astype(F32), 0.0).astype(BF)
    good = flags[...].astype(F32).astype(BF)
    terms = dot(weights, good).astype(BF)
    for j in range(NJ):
        masks[:, j * JW : (j + 1) * JW] = dot(good[:, j * BW : (j + 1) * BW], expand).astype(BF)
        for c in range(ND):
            blocks[c * NJ + j, :, JW:CW] = terms[:, j * BW : (j + 1) * BW]
    outs = []
    for c in range(ND):
        copies[2 + c].wait()
        for j in range(NJ):
            cols = slice(j * JW, (j + 1) * JW)
            blocks[c * NJ + j, :, 0:JW] = vis[c, :, cols] * masks[:, cols]
        part = pl.ds(c * NJ, NJ)
        outs.append(pltpu.make_async_copy(blocks.at[part], out_hbm.at[part], out_sems.at[c]))
        outs[-1].start()
    for copy in outs:
        copy.wait()


def pack(vis, flags, counts):
    return pl.pallas_call(
        pack_kernel,
        in_specs=[pl.BlockSpec(memory_space=pl.ANY)] * 3,
        out_specs=pl.BlockSpec(memory_space=pl.ANY),
        out_shape=jax.ShapeDtypeStruct((ND * NJ, TL, CW), BF),
        scratch_shapes=[
            pltpu.VMEM((ND, TL, 2 * NB), BF),
            pltpu.VMEM((TL, NB), jnp.int32),
            pltpu.VMEM((1, TL), jnp.int32),
            pltpu.VMEM((TL, 2 * NB), BF),
            pltpu.VMEM((ND * NJ, TL, CW), BF),
            pltpu.SemaphoreType.DMA((2 + ND,)),
            pltpu.SemaphoreType.DMA((ND,)),
        ],
        compiler_params=limit(8),
        name="pack",
    )(stay(vis), stay(flags), stay(counts))


def transform_kernel(got_ref, cols_ref, table_ref, proj_hbm, out_ref, proj_ref, data, sem):
    copy = pltpu.make_async_copy(proj_hbm, proj_ref, sem)
    copy.start()
    expand = spread()
    row, col = iota((JW, JW), 0), iota((JW, JW), 1)
    swap = jnp.where(row == col + 1, jnp.where(col % 2 == 0, 1.0, 0.0), 0.0)
    swap = swap - jnp.where(col == row + 1, jnp.where(col % 2 == 1, 1.0, 0.0), 0.0)
    swap = swap.astype(BF)
    for j in range(NJ):
        num = got_ref[j, :, 0:JW].astype(F32)
        den = got_ref[j, :, JW:CW].astype(F32)
        for d in range(1, ND):
            num += got_ref[d * NJ + j, :, 0:JW].astype(F32)
            den += got_ref[d * NJ + j, :, JW:CW].astype(F32)
        den = dot(jnp.maximum(den, 1.0).astype(BF), expand)
        averaged = (num / den).astype(BF)
        data[j * TL : (j + 1) * TL, :] = averaged
        data[TZ + j * TL : TZ + (j + 1) * TL, :] = dot(averaged, swap).astype(BF)
    part = dot(table_ref[...], data[...])
    part = (part * (1.0 / math.sqrt(NT))).astype(BF)
    one_hot = jnp.where(cols_ref[...] == iota((NM, NM), 1), 1.0, 0.0).astype(BF)
    rows = dot(one_hot, part)
    half = SKY * 8
    rest = jnp.concatenate([rows[half:, 0:NK], rows[half:, NK:]], axis=0).astype(BF)
    line = iota((half, 2 * NK), 0)
    place, device = line % 8, line // 8
    source = jnp.where(place < 2, 2 * device + place, jnp.where(place < 4, NK - 2 + 2 * device + place, -1))
    two = dot(jnp.where(source == iota((half, 2 * NK), 1), 1.0, 0.0).astype(BF), rest)
    blocks = [rows[0:half, 0:NK], rows[0:half, NK:], two]
    whole = jnp.concatenate([b.reshape(SKY, 8, NK) for b in blocks], axis=1)
    out_ref[...] = whole.reshape(SKY * PR, NK).astype(BF)
    copy.wait()


def transform(got, cols, table, projection):
    vmem, hbm = pl.BlockSpec(memory_space=pltpu.VMEM), pl.BlockSpec(memory_space=pl.ANY)
    return pl.pallas_call(
        transform_kernel,
        in_specs=[vmem, vmem, vmem, hbm],
        out_specs=[vmem, hbm],
        out_shape=[
            jax.ShapeDtypeStruct((SKY * PR, NK), BF),
            pltpu.VMEM((OS, 2 * NB, NK), BF),
        ],
        scratch_shapes=[pltpu.VMEM((2 * TZ, JW), BF), pltpu.SemaphoreType.DMA],
        compiler_params=limit(16),
        cost_estimate=pl.CostEstimate(flops=10**9, bytes_accessed=COST, transcendentals=0),
        name="transform",
    )(got, cols, table, stay(projection))


def project_kernel(parts_ref, proj, weight_ref, basis_hbm, out_ref, basis, mvis, turned, sems):
    basis_copies = [pltpu.make_async_copy(basis_hbm.at[s], basis.at[s], sems.at[s]) for s in range(OS)]
    for copy in basis_copies:
        copy.start()
    for j in range(NJ):
        y, c = j // NC, j % NC
        total = parts_ref[(y * NZ) * NC + c].astype(F32)
        for z in range(1, NZ):
            total += parts_ref[(y * NZ + z) * NC + c].astype(F32)
        low, high = slice(j * JW, j * JW + NK), slice(j * JW + NK, (j + 1) * JW)
        mvis[0:8, low] = total[0:8]
        mvis[0:8, high] = total[8:16]
        mvis[8:16, low] = total[16:24]
        mvis[8:16, high] = jnp.concatenate([total[18:24], total[16:18]], axis=0)
    left = mvis[...].astype(BF)
    slot = iota((SP, NK), 0)
    raw = jnp.zeros((SP, NK), F32)
    for s in range(OS):
        raw = jnp.where(slot == s, dot(left, proj[s]), raw)
    coef = (raw * weight_ref[...]).astype(BF)
    mode, row = iota((NK, 2 * NK), 0), iota((NK, 2 * NK), 1)
    left = [dot(coef, jnp.where(row == 2 * mode + q, 1.0, 0.0).astype(BF)) for q in range(2)]
    left = jnp.concatenate(left, axis=0).astype(BF)
    slot = iota((2 * SP, NR), 0) % SP
    profile = jnp.zeros((2 * SP, NR), F32)
    for s in range(OS):
        if s in (0, 4, 8):
            for copy in basis_copies[s : s + 4]:
                copy.wait()
        profile = jnp.where(slot == s, dot(left, basis[s].reshape(2 * NK, NR)), profile)
    turned[...] = profile.T
    pieces = [turned[pl.ds(r, SKY, stride=OR), :] for r in range(OR)]
    rows = [jnp.concatenate(pieces[4 * i : 4 * i + 4], axis=1) for i in range(EW // 128)]
    out_ref[...] = jnp.stack(rows, axis=1).astype(BF)


def project(parts, projection, weight, basis):
    vmem, hbm = pl.BlockSpec(memory_space=pltpu.VMEM), pl.BlockSpec(memory_space=pl.ANY)
    return pl.pallas_call(
        project_kernel,
        in_specs=[vmem, vmem, vmem, hbm],
        out_shape=jax.ShapeDtypeStruct((SKY, EW // 128, 128), BF),
        scratch_shapes=[
            pltpu.VMEM((OS, NK, 2, NR), BF),
            pltpu.VMEM((SP, 2 * NB), F32),
            pltpu.VMEM((NR, 2 * SP), F32),
            pltpu.SemaphoreType.DMA((OS,)),
        ],
        compiler_params=limit(20),
        cost_estimate=pl.CostEstimate(flops=10**9, bytes_accessed=COST, transcendentals=0),
        name="project",
    )(parts, projection, weight, stay(basis))


def nt(a, b):
    return lax.dot_general(a, b, (((1,), (1,)), ((), ())), preferred_element_type=F32)


def synthesis_kernel(got_ref, order_ref, table, out_ref, turned):
    got = got_ref[...].astype(F32)
    for i in range(EW // 128):
        turned[i * 128 : (i + 1) * 128, :] = got[:, i, :].T
    one_hot = jnp.where(iota((4 * QW, NM), 0) == order_ref[...], 1.0, 0.0).astype(BF)
    natural = []
    for q in range(2):
        pieces = [turned[pl.ds(q * SP + s, OR, stride=2 * SP), :] for s in range(OS)]
        slots = jnp.concatenate(pieces, axis=1).astype(BF)
        natural.append(nt(slots, one_hot).astype(BF))
    same, turn = [], []
    for r in range(4):
        real = natural[0][:, r * QW : r * QW + QM]
        imag = natural[1][:, r * QW : r * QW + QM]
        if r % 2 == 1:
            real, imag = jnp.concatenate([real, -imag], axis=0), jnp.concatenate([imag, real], axis=0)
        rows = 2 * r * QM
        both = dot(real, table[rows : rows + QM, :]) + dot(imag, table[rows + QM : rows + 2 * QM, :])
        same.append(both[0:OR])
        turn.append(both[OR:])
    quarters = [
        same[0] + same[2] + (same[1] + same[3]),
        same[0] - same[2] + (turn[1] - turn[3]),
        same[0] + same[2] - (same[1] + same[3]),
        same[0] - same[2] - (turn[1] - turn[3]),
    ]
    for k in range(4):
        out_ref[:, k * NPHI // 4 : (k + 1) * NPHI // 4] = quarters[k] * (1.0 / math.sqrt(NM))


def synthesis(got, order, table):
    vmem = pl.BlockSpec(memory_space=pltpu.VMEM)
    return pl.pallas_call(
        synthesis_kernel,
        out_shape=jax.ShapeDtypeStruct((OR, NPHI), F32),
        scratch_shapes=[
            pltpu.VMEM((EW, SKY), F32),
        ],
        compiler_params=limit(8),
        name="synthesis",
    )(got, order, table)


def body(visibility, flags, counts, m_order, projection, singular, cycles_basis):
    sky = ("y", "z", "core")
    sent = pack(visibility[0], flags[0], counts)
    got = lax.all_to_all(sent, ("day", "y", "core"), split_axis=0, concat_axis=0, tiled=True)
    slots = m_order.reshape(SKY, OS)
    cols = jnp.concatenate([slots[:, 0:8].reshape(-1, 1), slots[:, 8:].reshape(-1, 1)], axis=0)
    places = slots % 4 * QW + slots // 4
    places = places.T.reshape(1, NM)
    table = lax.dynamic_index_in_dim(transform_table(), lax.axis_index("z"), 0, keepdims=False)
    own = lax.dynamic_slice_in_dim(m_order, lax.axis_index(sky) * OS, OS)
    rank = NK - NK * own // (2 * NM)
    keep = jnp.arange(NK, dtype=jnp.int32)[None, :] < rank[:, None]
    sing = singular[0]
    weight = jnp.where(keep, sing / (sing * sing + 0.25), 0.0)
    weight = jnp.pad(weight, ((0, SP - OS), (0, 0)))
    got, table, cols, places, weight = lax.optimization_barrier((got, table, cols, places, weight))
    packed, held = transform(got, cols, table, projection[0])
    packed = packed.reshape(SKY, PR, NK)
    parts = lax.all_to_all(packed, sky, split_axis=0, concat_axis=0, tiled=True)
    blocks = project(parts, held, weight, cycles_basis[0])
    gathered = lax.all_to_all(blocks, sky, split_axis=0, concat_axis=0, tiled=True)
    return synthesis(gathered, places, jnp.asarray(synthesis_table()))[None]


def solution(mesh):
    fine = Mesh(mesh.devices.reshape(ND, NY, NZ, NC), ("day", "y", "z", "core"))
    sky = ("y", "z", "core")
    return jax.shard_map(
        body,
        mesh=fine,
        in_specs=(
            P("day", None, sky, None),
            P("day", sky, None),
            P("day", sky),
            P(),
            P("day", sky, None, None),
            P("day", sky, None),
            P("day", sky, None, None, None),
        ),
        out_specs=P("day", sky, None),
        check_vma=False,
    )
```

```python
import math

import jax
import jax.numpy as jnp
import ml_dtypes
import numpy as np
from jax import lax
from jax.experimental import pallas as pl
from jax.experimental.pallas import tpu as pltpu
from jax.sharding import Mesh
from jax.sharding import PartitionSpec as P

NB, NT, NM, NK, NR, NPHI = 1024, 4096, 640, 128, 1024, 2048
ND, NY, NZ, NC = 4, 4, 8, 2
SKY = NY * NZ * NC
NJ = NY * NC
JW = 2 * NB // NJ
BW = NB // NJ
TL = NT // SKY
TQ = TL * NC
OS = NM // SKY
OR = NR // SKY
CW = JW + BW
PR = 24
QM = NM // 4
QW = 256
SP = 16
EW = 2 * SP * OR
MIB = 1024 * 1024
HIDE = 3 * 10**9
BF, F32 = jnp.bfloat16, jnp.float32


def transform_table():
    m = np.arange(NM).reshape(QM, 4).T.reshape(1, NM, 1)
    z, c, t = np.ix_(np.arange(NZ), np.arange(NC), np.arange(TL))
    times = ((z * NC + c) * TL + t).reshape(NZ, 1, NC * TL)
    angle = (m * times % NT) * (2.0 * math.pi / NT)
    return np.concatenate([np.cos(angle), np.sin(angle)], axis=2).astype(ml_dtypes.bfloat16)


def synthesis_table():
    p = np.arange(NPHI // 4)[None, :]
    out = np.zeros((4, 2, QM, NPHI // 4))
    for r in range(4):
        angle = (np.arange(r, NM, 4)[:, None] * p % NPHI) * (2.0 * math.pi / NPHI)
        out[r, 0], out[r, 1] = np.cos(angle), -np.sin(angle)
    return out.reshape(8 * QM, NPHI // 4).astype(ml_dtypes.bfloat16)


def iota(shape, dim):
    return lax.broadcasted_iota(jnp.int32, shape, dim)


def spread():
    return jnp.where(iota((BW, JW), 0) == iota((BW, JW), 1) // 2, 1.0, 0.0).astype(BF)


def dot(a, b):
    return jnp.dot(a, b, preferred_element_type=F32)


def limit(mib):
    return pltpu.CompilerParams(vmem_limit_bytes=mib * MIB)


def stay(x):
    return pltpu.with_memory_space_constraint(x, pltpu.HBM)


def pack_kernel(vis_hbm, flags_hbm, counts_hbm, out_hbm, vis, flags, counts, masks, blocks, sems, out_sems):
    copies = [
        pltpu.make_async_copy(flags_hbm, flags, sems.at[0]),
        pltpu.make_async_copy(counts_hbm, counts, sems.at[1]),
    ] + [pltpu.make_async_copy(vis_hbm.at[c], vis.at[c], sems.at[2 + c]) for c in range(ND)]
    for copy in copies:
        copy.start()
    expand = spread()
    eye = iota((TL, TL), 0) == iota((TL, TL), 1)
    copies[0].wait()
    copies[1].wait()
    weights = jnp.where(eye, counts[...].astype(F32), 0.0).astype(BF)
    good = flags[...].astype(F32).astype(BF)
    terms = dot(weights, good).astype(BF)
    for j in range(NJ):
        masks[:, j * JW : (j + 1) * JW] = dot(good[:, j * BW : (j + 1) * BW], expand).astype(BF)
        for c in range(ND):
            blocks[c * NJ + j, :, JW:CW] = terms[:, j * BW : (j + 1) * BW]
    outs = []
    for c in range(ND):
        copies[2 + c].wait()
        for j in range(NJ):
            cols = slice(j * JW, (j + 1) * JW)
            blocks[c * NJ + j, :, 0:JW] = vis[c, :, cols] * masks[:, cols]
        part = pl.ds(c * NJ, NJ)
        outs.append(pltpu.make_async_copy(blocks.at[part], out_hbm.at[part], out_sems.at[c]))
        outs[-1].start()
    for copy in outs:
        copy.wait()


def pack(vis, flags, counts):
    return pl.pallas_call(
        pack_kernel,
        in_specs=[pl.BlockSpec(memory_space=pl.ANY)] * 3,
        out_specs=pl.BlockSpec(memory_space=pl.ANY),
        out_shape=jax.ShapeDtypeStruct((ND * NJ, TL, CW), BF),
        scratch_shapes=[
            pltpu.VMEM((ND, TL, 2 * NB), BF),
            pltpu.VMEM((TL, NB), jnp.int32),
            pltpu.VMEM((1, TL), jnp.int32),
            pltpu.VMEM((TL, 2 * NB), BF),
            pltpu.VMEM((ND * NJ, TL, CW), BF),
            pltpu.SemaphoreType.DMA((2 + ND,)),
            pltpu.SemaphoreType.DMA((ND,)),
        ],
        compiler_params=limit(8),
        name="pack",
    )(stay(vis), stay(flags), stay(counts))


def transform_kernel(got_ref, cols_ref, table_ref, out_ref, data):
    expand = spread()
    row, col = iota((JW, JW), 0), iota((JW, JW), 1)
    swap = jnp.where(row == col + 1, jnp.where(col % 2 == 0, 1.0, 0.0), 0.0)
    swap = swap - jnp.where(col == row + 1, jnp.where(col % 2 == 1, 1.0, 0.0), 0.0)
    swap = swap.astype(BF)
    values, turned = [], []
    for j in range(NJ):
        num = got_ref[j, :, 0:JW].astype(F32)
        den = got_ref[j, :, JW:CW].astype(F32)
        for d in range(1, ND):
            num += got_ref[d * NJ + j, :, 0:JW].astype(F32)
            den += got_ref[d * NJ + j, :, JW:CW].astype(F32)
        den = dot(jnp.maximum(den, 1.0).astype(BF), expand)
        averaged = (num / den).astype(BF)
        values.append(averaged.astype(F32))
        turned.append(dot(averaged, swap))
    for c in range(NC):
        v, t = values[c::NC], turned[c::NC]
        even, odd = v[0] + v[2], v[1] + v[3]
        even_t, odd_t = t[0] + t[2], t[1] + t[3]
        less, rest = v[0] - v[2], v[1] - v[3]
        less_t, rest_t = t[0] - t[2], t[1] - t[3]
        sums = [
            (even + odd, even_t + odd_t),
            (less + rest_t, less_t - rest),
            (even - odd, even_t - odd_t),
            (less - rest_t, less_t + rest),
        ]
        for r in range(4):
            for k in range(2):
                row = (2 * r + k) * TQ + c * TL
                data[row : row + TL, :] = sums[r][k].astype(BF)
    parts = [
        dot(table_ref[r * QM : (r + 1) * QM, :], data[2 * r * TQ : 2 * (r + 1) * TQ, :]) for r in range(4)
    ]
    part = (jnp.concatenate(parts, axis=0) * (1.0 / math.sqrt(NT))).astype(BF)
    one_hot = jnp.where(cols_ref[...] == iota((NM, NM), 1), 1.0, 0.0).astype(BF)
    rows = dot(one_hot, part)
    half = SKY * 8
    rest = jnp.concatenate([rows[half:, 0:NK], rows[half:, NK:]], axis=0).astype(BF)
    line = iota((half, 2 * NK), 0)
    place, device = line % 8, line // 8
    source = jnp.where(place < 2, 2 * device + place, jnp.where(place < 4, NK - 2 + 2 * device + place, -1))
    two = dot(jnp.where(source == iota((half, 2 * NK), 1), 1.0, 0.0).astype(BF), rest)
    blocks = [rows[0:half, 0:NK], rows[0:half, NK:], two]
    whole = jnp.concatenate([b.reshape(SKY, 8, NK) for b in blocks], axis=1)
    out_ref[...] = whole.reshape(SKY * PR, NK).astype(BF)


def transform(got, cols, table):
    return pl.pallas_call(
        transform_kernel,
        out_shape=jax.ShapeDtypeStruct((SKY * PR, NK), BF),
        scratch_shapes=[pltpu.VMEM((8 * TQ, JW), BF)],
        compiler_params=limit(8),
        cost_estimate=pl.CostEstimate(flops=HIDE, bytes_accessed=HIDE // 300, transcendentals=0),
        name="transform",
    )(got, cols, table)


def project_kernel(parts_ref, proj, weight_ref, basis, out_ref, mvis, turned, packed):
    for j in range(NJ):
        y, c = j // NC, j % NC
        total = parts_ref[(y * NZ) * NC + c].astype(F32)
        for z in range(1, NZ):
            total += parts_ref[(y * NZ + z) * NC + c].astype(F32)
        low, high = slice(j * JW, j * JW + NK), slice(j * JW + NK, (j + 1) * JW)
        mvis[0:8, low] = total[0:8]
        mvis[0:8, high] = total[8:16]
        mvis[8:16, low] = total[16:24]
        mvis[8:16, high] = jnp.concatenate([total[18:24], total[16:18]], axis=0)
    left = mvis[...].astype(BF)
    slot = iota((SP, NK), 0)
    raw = jnp.zeros((SP, NK), F32)
    for s in range(OS):
        raw = jnp.where(slot == s, dot(left, proj[s]), raw)
    coef = (raw * weight_ref[...]).astype(BF)
    mode, row = iota((NK, 2 * NK), 0), iota((NK, 2 * NK), 1)
    left = [dot(coef, jnp.where(row == 2 * mode + q, 1.0, 0.0).astype(BF)) for q in range(2)]
    left = jnp.concatenate(left, axis=0).astype(BF)
    slot = iota((2 * SP, NR), 0) % SP
    profile = jnp.zeros((2 * SP, NR), F32)
    for s in range(OS):
        profile = jnp.where(slot == s, dot(left, basis[s].reshape(2 * NK, NR)), profile)
    turned[...] = profile.T
    pieces = [turned[pl.ds(r, SKY, stride=OR), :] for r in range(OR)]
    lines = EW // 128
    for i in range(lines):
        packed[pl.ds(i, SKY, stride=lines), :] = jnp.concatenate(pieces[4 * i : 4 * i + 4], axis=1)
    out_ref[...] = packed[...].astype(BF)


def project(parts, projection, weight, basis):
    return pl.pallas_call(
        project_kernel,
        out_shape=jax.ShapeDtypeStruct((SKY * EW // 128, 128), BF),
        scratch_shapes=[
            pltpu.VMEM((SP, 2 * NB), F32),
            pltpu.VMEM((NR, 2 * SP), F32),
            pltpu.VMEM((SKY * EW // 128, 128), F32),
        ],
        compiler_params=limit(8),
        name="project",
    )(parts, projection, weight, basis)


def nt(a, b):
    return lax.dot_general(a, b, (((1,), (1,)), ((), ())), preferred_element_type=F32)


def synthesis_kernel(got_ref, order_ref, table, out_ref, turned):
    got = got_ref[...].astype(F32)
    for i in range(EW // 128):
        turned[i * 128 : (i + 1) * 128, :] = got[:, i, :].T
    one_hot = jnp.where(iota((4 * QW, NM), 0) == order_ref[...], 1.0, 0.0).astype(BF)
    natural = []
    for q in range(2):
        pieces = [turned[pl.ds(q * SP + s, OR, stride=2 * SP), :] for s in range(OS)]
        slots = jnp.concatenate(pieces, axis=1).astype(BF)
        natural.append(nt(slots, one_hot).astype(BF))
    same, turn = [], []
    for r in range(4):
        real = natural[0][:, r * QW : r * QW + QM]
        imag = natural[1][:, r * QW : r * QW + QM]
        if r % 2 == 1:
            real, imag = jnp.concatenate([real, -imag], axis=0), jnp.concatenate([imag, real], axis=0)
        rows = 2 * r * QM
        both = dot(real, table[rows : rows + QM, :]) + dot(imag, table[rows + QM : rows + 2 * QM, :])
        same.append(both[0:OR])
        turn.append(both[OR:])
    quarters = [
        same[0] + same[2] + (same[1] + same[3]),
        same[0] - same[2] + (turn[1] - turn[3]),
        same[0] + same[2] - (same[1] + same[3]),
        same[0] - same[2] - (turn[1] - turn[3]),
    ]
    for k in range(4):
        out_ref[:, k * NPHI // 4 : (k + 1) * NPHI // 4] = quarters[k] * (1.0 / math.sqrt(NM))


def synthesis(got, order, table):
    vmem = pl.BlockSpec(memory_space=pltpu.VMEM)
    return pl.pallas_call(
        synthesis_kernel,
        out_shape=jax.ShapeDtypeStruct((OR, NPHI), F32),
        scratch_shapes=[
            pltpu.VMEM((EW, SKY), F32),
        ],
        compiler_params=limit(8),
        name="synthesis",
    )(got, order, table)


def body(visibility, flags, counts, m_order, projection, singular, cycles_basis):
    sky = ("y", "z", "core")
    sent = pack(visibility[0], flags[0], counts)
    got = lax.all_to_all(sent, ("day", "y", "core"), split_axis=0, concat_axis=0, tiled=True)
    slots = m_order.reshape(SKY, OS)
    lines = slots % 4 * QM + slots // 4
    cols = jnp.concatenate([lines[:, 0:8].reshape(-1, 1), lines[:, 8:].reshape(-1, 1)], axis=0)
    places = slots % 4 * QW + slots // 4
    places = places.T.reshape(1, NM)
    table = lax.dynamic_index_in_dim(transform_table(), lax.axis_index("z"), 0, keepdims=False)
    own = lax.dynamic_slice_in_dim(m_order, lax.axis_index(sky) * OS, OS)
    rank = NK - NK * own // (2 * NM)
    keep = jnp.arange(NK, dtype=jnp.int32)[None, :] < rank[:, None]
    sing = singular[0]
    weight = jnp.where(keep, sing / (sing * sing + 0.25), 0.0)
    weight = jnp.pad(weight, ((0, SP - OS), (0, 0)))
    got, table, cols, places, weight = lax.optimization_barrier((got, table, cols, places, weight))
    packed = transform(got, cols, table)
    packed = packed.reshape(SKY, PR, NK)
    parts = lax.all_to_all(packed, sky, split_axis=0, concat_axis=0, tiled=True)
    blocks = project(parts, projection[0], weight, cycles_basis[0]).reshape(SKY, EW // 128, 128)
    gathered = lax.all_to_all(blocks, sky, split_axis=0, concat_axis=0, tiled=True)
    return synthesis(gathered, places, jnp.asarray(synthesis_table()))[None]


def solution(mesh):
    fine = Mesh(mesh.devices.reshape(ND, NY, NZ, NC), ("day", "y", "z", "core"))
    sky = ("y", "z", "core")
    return jax.shard_map(
        body,
        mesh=fine,
        in_specs=(
            P("day", None, sky, None),
            P("day", sky, None),
            P("day", sky),
            P(),
            P("day", sky, None, None),
            P("day", sky, None),
            P("day", sky, None, None, None),
        ),
        out_specs=P("day", sky, None),
        check_vma=False,
    )
```

```python
import math

import jax
import jax.numpy as jnp
import ml_dtypes
import numpy as np
from jax import lax
from jax.experimental import pallas as pl
from jax.experimental.pallas import tpu as pltpu
from jax.sharding import Mesh
from jax.sharding import PartitionSpec as P

NB, NT, NM, NK, NR, NPHI = 1024, 4096, 640, 128, 1024, 2048
ND, NY, NZ, NC = 4, 4, 8, 2
SKY = NY * NZ * NC
NJ = NY
JW = 2 * NB // NJ
BW = NB // NJ
SW = 256
TL = NT // SKY
OS = NM // SKY
OR = NR // SKY
CW = JW + BW
NP = NY * NZ
PR = 40
QM = NM // 4
QW = 256
SP = 16
EW = 2 * SP * OR
MIB = 1024 * 1024
HIDE = 3 * 10**9
BF, F32 = jnp.bfloat16, jnp.float32


def transform_table():
    m = np.arange(NM).reshape(QM, 4).T.reshape(1, NM, 1)
    z, c, other, t = np.ix_(np.arange(NZ), np.arange(NC), np.arange(2), np.arange(TL))
    times = ((z * NC + (c + other) % NC) * TL + t).reshape(NZ * NC, 1, 2, TL)
    angle = (m[..., None] * times % NT) * (2.0 * math.pi / NT)
    table = np.stack([np.cos(angle), np.sin(angle)], axis=3)
    return table.reshape(NZ * NC, NM, 4 * TL).astype(ml_dtypes.bfloat16)


def synthesis_table():
    p = np.arange(NPHI // 4)[None, :]
    out = np.zeros((4, 2, QM, NPHI // 4))
    for r in range(4):
        angle = (np.arange(r, NM, 4)[:, None] * p % NPHI) * (2.0 * math.pi / NPHI)
        out[r, 0], out[r, 1] = np.cos(angle), -np.sin(angle)
    return out.reshape(8 * QM, NPHI // 4).astype(ml_dtypes.bfloat16)


def iota(shape, dim):
    return lax.broadcasted_iota(jnp.int32, shape, dim)


def spread():
    return jnp.where(iota((SW // 2, SW), 0) == iota((SW // 2, SW), 1) // 2, 1.0, 0.0).astype(BF)


def turn(x):
    row, col = iota((SW, SW), 0), iota((SW, SW), 1)
    swap = jnp.where(row == col + 1, jnp.where(col % 2 == 0, 1.0, 0.0), 0.0)
    swap = swap - jnp.where(col == row + 1, jnp.where(col % 2 == 1, 1.0, 0.0), 0.0)
    swap = swap.astype(BF)
    return jnp.concatenate([dot(x[:, k : k + SW], swap) for k in range(0, JW, SW)], axis=1)


def dot(a, b):
    return jnp.dot(a, b, preferred_element_type=F32)


def limit(mib):
    return pltpu.CompilerParams(vmem_limit_bytes=mib * MIB)


def stay(x):
    return pltpu.with_memory_space_constraint(x, pltpu.HBM)


def pack_kernel(vis_hbm, flags_hbm, counts_hbm, out_hbm, vis, flags, counts, masks, blocks, sems, out_sems):
    copies = [
        pltpu.make_async_copy(flags_hbm, flags, sems.at[0]),
        pltpu.make_async_copy(counts_hbm, counts, sems.at[1]),
    ] + [pltpu.make_async_copy(vis_hbm.at[c], vis.at[c], sems.at[2 + c]) for c in range(ND)]
    for copy in copies:
        copy.start()
    expand = spread()
    eye = iota((TL, TL), 0) == iota((TL, TL), 1)
    copies[0].wait()
    copies[1].wait()
    weights = jnp.where(eye, counts[...].astype(F32), 0.0).astype(BF)
    good = flags[...].astype(F32).astype(BF)
    terms = dot(weights, good).astype(BF)
    for k in range(2 * NB // SW):
        masks[:, k * SW : (k + 1) * SW] = dot(good[:, k * SW // 2 : (k + 1) * SW // 2], expand).astype(BF)
    for j in range(NJ):
        for c in range(ND):
            blocks[c * NJ + j, :, JW:CW] = terms[:, j * BW : (j + 1) * BW]
    outs = []
    for c in range(ND):
        copies[2 + c].wait()
        for j in range(NJ):
            cols = slice(j * JW, (j + 1) * JW)
            blocks[c * NJ + j, :, 0:JW] = vis[c, :, cols] * masks[:, cols]
            outs.append(pltpu.make_async_copy(blocks.at[c * NJ + j], out_hbm.at[c * NJ + j], out_sems.at[c, j]))
            outs[-1].start()
    for copy in outs:
        copy.wait()


def pack(vis, flags, counts):
    return pl.pallas_call(
        pack_kernel,
        in_specs=[pl.BlockSpec(memory_space=pl.ANY)] * 3,
        out_specs=pl.BlockSpec(memory_space=pl.ANY),
        out_shape=jax.ShapeDtypeStruct((ND * NJ, TL, CW), BF),
        scratch_shapes=[
            pltpu.VMEM((ND, TL, 2 * NB), BF),
            pltpu.VMEM((TL, NB), jnp.int32),
            pltpu.VMEM((1, TL), jnp.int32),
            pltpu.VMEM((TL, 2 * NB), BF),
            pltpu.VMEM((ND * NJ, TL, CW), BF),
            pltpu.SemaphoreType.DMA((2 + ND,)),
            pltpu.SemaphoreType.DMA((ND, NJ)),
        ],
        compiler_params=limit(8),
        name="pack",
    )(stay(vis), stay(flags), stay(counts))


def average_kernel(got_ref, out_ref):
    expand = spread()
    values, turned = [], []
    for y in range(NY):
        num = got_ref[y, :, 0:JW].astype(F32)
        den = got_ref[y, :, JW:CW].astype(F32)
        for d in range(1, ND):
            num += got_ref[d * NY + y, :, 0:JW].astype(F32)
            den += got_ref[d * NY + y, :, JW:CW].astype(F32)
        den = jnp.maximum(den, 1.0).astype(BF)
        den = jnp.concatenate([dot(den[:, k : k + SW // 2], expand) for k in range(0, BW, SW // 2)], axis=1)
        averaged = (num / den).astype(BF)
        values.append(averaged.astype(F32))
        turned.append(turn(averaged) if y % 2 == 1 else None)
    even, odd = values[0] + values[2], values[1] + values[3]
    less, rest = values[0] - values[2], turned[1] - turned[3]
    sums = [even + odd, less + rest, even - odd, less - rest]
    for r in range(4):
        out_ref[r * TL : (r + 1) * TL, :] = sums[r].astype(BF)


def average(got):
    return pl.pallas_call(
        average_kernel,
        out_shape=jax.ShapeDtypeStruct((4 * TL, JW), BF),
        compiler_params=limit(8),
        name="average",
    )(got)


def half_kernel(sums_ref, table_ref, out_ref):
    for r in range(4):
        x = sums_ref[r * TL : (r + 1) * TL, :]
        data = jnp.concatenate([x, turn(x).astype(BF)], axis=0)
        out_ref[r * QM : (r + 1) * QM, :] = dot(table_ref[r * QM : (r + 1) * QM, 0 : 2 * TL], data)


def half(sums, table):
    return pl.pallas_call(
        half_kernel,
        out_shape=jax.ShapeDtypeStruct((NM, JW), F32),
        compiler_params=limit(8),
        cost_estimate=pl.CostEstimate(flops=10**9, bytes_accessed=10**7, transcendentals=0),
        name="half",
    )(sums, table)


def transform_kernel(sums_ref, table_ref, half_ref, cols_ref, out_ref):
    parts = []
    for r in range(4):
        x = sums_ref[r * TL : (r + 1) * TL, :]
        data = jnp.concatenate([x, turn(x).astype(BF)], axis=0)
        parts.append(dot(table_ref[r * QM : (r + 1) * QM, 2 * TL : 4 * TL], data))
    part = jnp.concatenate(parts, axis=0) + half_ref[...]
    part = (part * (1.0 / math.sqrt(NT))).astype(BF)
    one_hot = jnp.where(cols_ref[...] == iota((NP * OS, NM), 1), 1.0, 0.0).astype(BF)
    rows = dot(one_hot, part)
    eight, groups = NP * 8, JW // NK
    first = [rows[0:eight, g * NK : (g + 1) * NK] for g in range(groups)]
    rest = [rows[eight:, g * NK : (g + 1) * NK] for g in range(groups)]
    rest = jnp.concatenate(rest, axis=0).astype(BF)
    line = iota((eight, groups * 2 * NP), 0)
    place, device = line % 8, line // 8
    source = place // 2 * (2 * NP) + 2 * device + place % 2
    last = dot(jnp.where(source == iota((eight, groups * 2 * NP), 1), 1.0, 0.0).astype(BF), rest)
    whole = jnp.concatenate([b.reshape(NP, 8, NK) for b in first + [last]], axis=1)
    out_ref[...] = whole.reshape(NP * PR, NK).astype(BF)


def transform(sums, table, own, cols):
    return pl.pallas_call(
        transform_kernel,
        out_shape=jax.ShapeDtypeStruct((NP * PR, NK), BF),
        compiler_params=limit(8),
        cost_estimate=pl.CostEstimate(flops=HIDE, bytes_accessed=HIDE // 300, transcendentals=0),
        name="transform",
    )(sums, table, own, cols)


def project_kernel(parts_ref, proj, weight_ref, basis, out_ref, mvis, turned, packed):
    for y in range(NY):
        total = parts_ref[y].astype(F32)
        for z in range(1, NZ):
            total += parts_ref[z * NY + y].astype(F32)
        for g in range(JW // NK):
            cols = slice(y * JW + g * NK, y * JW + (g + 1) * NK)
            mvis[0:8, cols] = total[8 * g : 8 * g + 8]
            last = total[32 + 2 * g : 34 + 2 * g]
            mvis[8:16, cols] = jnp.concatenate([last, jnp.zeros((6, NK), F32)], axis=0)
    left = mvis[...].astype(BF)
    slot = iota((SP, NK), 0)
    raw = jnp.zeros((SP, NK), F32)
    for s in range(OS):
        raw = jnp.where(slot == s, dot(left, proj[s]), raw)
    coef = (raw * weight_ref[...]).astype(BF)
    mode, row = iota((NK, 2 * NK), 0), iota((NK, 2 * NK), 1)
    left = [dot(coef, jnp.where(row == 2 * mode + q, 1.0, 0.0).astype(BF)) for q in range(2)]
    left = jnp.concatenate(left, axis=0).astype(BF)
    slot = iota((2 * SP, NR), 0) % SP
    profile = jnp.zeros((2 * SP, NR), F32)
    for s in range(OS):
        profile = jnp.where(slot == s, dot(left, basis[s].reshape(2 * NK, NR)), profile)
    turned[...] = profile.T
    pieces = [turned[pl.ds(r, SKY, stride=OR), :] for r in range(OR)]
    lines = EW // 128
    for i in range(lines):
        packed[pl.ds(i, SKY, stride=lines), :] = jnp.concatenate(pieces[4 * i : 4 * i + 4], axis=1)
    out_ref[...] = packed[...].astype(BF)


def project(parts, projection, weight, basis):
    return pl.pallas_call(
        project_kernel,
        out_shape=jax.ShapeDtypeStruct((SKY * EW // 128, 128), BF),
        scratch_shapes=[
            pltpu.VMEM((SP, 2 * NB), F32),
            pltpu.VMEM((NR, 2 * SP), F32),
            pltpu.VMEM((SKY * EW // 128, 128), F32),
        ],
        compiler_params=limit(8),
        name="project",
    )(parts, projection, weight, basis)


def nt(a, b):
    return lax.dot_general(a, b, (((1,), (1,)), ((), ())), preferred_element_type=F32)


def synthesis_kernel(got_ref, order_ref, table, out_ref, turned):
    got = got_ref[...].astype(F32)
    for i in range(EW // 128):
        turned[i * 128 : (i + 1) * 128, :] = got[:, i, :].T
    one_hot = jnp.where(iota((4 * QW, NM), 0) == order_ref[...], 1.0, 0.0).astype(BF)
    natural = []
    for q in range(2):
        pieces = [turned[pl.ds(q * SP + s, OR, stride=2 * SP), :] for s in range(OS)]
        slots = jnp.concatenate(pieces, axis=1).astype(BF)
        natural.append(nt(slots, one_hot).astype(BF))
    same, turn = [], []
    for r in range(4):
        real = natural[0][:, r * QW : r * QW + QM]
        imag = natural[1][:, r * QW : r * QW + QM]
        if r % 2 == 1:
            real, imag = jnp.concatenate([real, -imag], axis=0), jnp.concatenate([imag, real], axis=0)
        rows = 2 * r * QM
        both = dot(real, table[rows : rows + QM, :]) + dot(imag, table[rows + QM : rows + 2 * QM, :])
        same.append(both[0:OR])
        turn.append(both[OR:])
    quarters = [
        same[0] + same[2] + (same[1] + same[3]),
        same[0] - same[2] + (turn[1] - turn[3]),
        same[0] + same[2] - (same[1] + same[3]),
        same[0] - same[2] - (turn[1] - turn[3]),
    ]
    for k in range(4):
        out_ref[:, k * NPHI // 4 : (k + 1) * NPHI // 4] = quarters[k] * (1.0 / math.sqrt(NM))


def synthesis(got, order, table):
    vmem = pl.BlockSpec(memory_space=pltpu.VMEM)
    return pl.pallas_call(
        synthesis_kernel,
        out_shape=jax.ShapeDtypeStruct((OR, NPHI), F32),
        scratch_shapes=[
            pltpu.VMEM((EW, SKY), F32),
        ],
        compiler_params=limit(8),
        name="synthesis",
    )(got, order, table)


def body(visibility, flags, counts, m_order, projection, singular, cycles_basis):
    sky = ("y", "z", "core")
    sent = pack(visibility[0], flags[0], counts)
    got = lax.all_to_all(sent, ("day", "y"), split_axis=0, concat_axis=0, tiled=True)
    slots = m_order.reshape(SKY, OS)
    lines = slots % 4 * QM + slots // 4
    core = lax.axis_index("core")
    lines = lax.dynamic_index_in_dim(lines.reshape(NY, NZ, NC, OS), core, 2, keepdims=False)
    lines = lines.transpose(1, 0, 2).reshape(NP, OS)
    cols = jnp.concatenate([lines[:, 0:8].reshape(-1, 1), lines[:, 8:].reshape(-1, 1)], axis=0)
    places = slots % 4 * QW + slots // 4
    places = places.T.reshape(1, NM)
    table = lax.dynamic_index_in_dim(transform_table(), lax.axis_index("z") * NC + core, 0, keepdims=False)
    own = lax.dynamic_slice_in_dim(m_order, lax.axis_index(sky) * OS, OS)
    rank = NK - NK * own // (2 * NM)
    keep = jnp.arange(NK, dtype=jnp.int32)[None, :] < rank[:, None]
    sing = singular[0]
    weight = jnp.where(keep, sing / (sing * sing + 0.25), 0.0)
    weight = jnp.pad(weight, ((0, SP - OS), (0, 0)))
    got, table, cols, places, weight = lax.optimization_barrier((got, table, cols, places, weight))
    sums = average(got)
    others = lax.ppermute(sums, "core", [(0, 1), (1, 0)])
    packed = transform(others, table, half(sums, table), cols).reshape(NP, PR, NK)
    parts = lax.all_to_all(packed, ("z", "y"), split_axis=0, concat_axis=0, tiled=True)
    blocks = project(parts, projection[0], weight, cycles_basis[0]).reshape(SKY, EW // 128, 128)
    gathered = lax.all_to_all(blocks, sky, split_axis=0, concat_axis=0, tiled=True)
    return synthesis(gathered, places, jnp.asarray(synthesis_table()))[None]


def solution(mesh):
    fine = Mesh(mesh.devices.reshape(ND, NY, NZ, NC), ("day", "y", "z", "core"))
    sky = ("y", "z", "core")
    return jax.shard_map(
        body,
        mesh=fine,
        in_specs=(
            P("day", None, sky, None),
            P("day", sky, None),
            P("day", sky),
            P(),
            P("day", sky, None, None),
            P("day", sky, None),
            P("day", sky, None, None, None),
        ),
        out_specs=P("day", sky, None),
        check_vma=False,
    )
```

```python
import math

import jax
import jax.numpy as jnp
import ml_dtypes
import numpy as np
from jax import lax
from jax.experimental import pallas as pl
from jax.experimental.pallas import tpu as pltpu
from jax.sharding import Mesh
from jax.sharding import PartitionSpec as P

NB, NT, NM, NK, NR, NPHI = 1024, 4096, 640, 128, 1024, 2048
ND, NY, NZ, NC = 4, 4, 8, 2
SKY = NY * NZ * NC
NJ = NY
JW = 2 * NB // NJ
BW = NB // NJ
SW = 256
TL = NT // SKY
OS = NM // SKY
OR = NR // SKY
NP = NY * NZ
PR = 40
QM = NM // 4
QW = 256
SP = 16
EW = 2 * SP * OR
MIB = 1024 * 1024
HIDE = 3 * 10**9
BF, F32 = jnp.bfloat16, jnp.float32


def transform_table():
    m = np.arange(NM).reshape(QM, 4).T.reshape(1, NM, 1)
    z, c, other, t = np.ix_(np.arange(NZ), np.arange(NC), np.arange(2), np.arange(TL))
    times = ((z * NC + (c + other) % NC) * TL + t).reshape(NZ * NC, 1, 2, TL)
    angle = (m[..., None] * times % NT) * (2.0 * math.pi / NT)
    table = np.stack([np.cos(angle), np.sin(angle)], axis=3)
    return table.reshape(NZ * NC, NM, 4 * TL).astype(ml_dtypes.bfloat16)


def synthesis_table():
    p = np.arange(NPHI // 4)[None, :]
    out = np.zeros((4, 2, QM, NPHI // 4))
    for r in range(4):
        angle = (np.arange(r, NM, 4)[:, None] * p % NPHI) * (2.0 * math.pi / NPHI)
        out[r, 0], out[r, 1] = np.cos(angle), -np.sin(angle)
    return out.reshape(8 * QM, NPHI // 4).astype(ml_dtypes.bfloat16)


def iota(shape, dim):
    return lax.broadcasted_iota(jnp.int32, shape, dim)


def spread():
    return jnp.where(iota((SW // 2, SW), 0) == iota((SW // 2, SW), 1) // 2, 1.0, 0.0).astype(BF)


def turn(x):
    row, col = iota((SW, SW), 0), iota((SW, SW), 1)
    swap = jnp.where(row == col + 1, jnp.where(col % 2 == 0, 1.0, 0.0), 0.0)
    swap = swap - jnp.where(col == row + 1, jnp.where(col % 2 == 1, 1.0, 0.0), 0.0)
    swap = swap.astype(BF)
    return jnp.concatenate([dot(x[:, k : k + SW], swap) for k in range(0, JW, SW)], axis=1)


def dot(a, b):
    return jnp.dot(a, b, preferred_element_type=F32)


def limit(mib):
    return pltpu.CompilerParams(vmem_limit_bytes=mib * MIB)


def stay(x):
    return pltpu.with_memory_space_constraint(x, pltpu.HBM)


def weigh_kernel(flags_hbm, counts_hbm, terms_ref, masks_ref, flags, counts, sems):
    copies = [
        pltpu.make_async_copy(flags_hbm, flags, sems.at[0]),
        pltpu.make_async_copy(counts_hbm, counts, sems.at[1]),
    ]
    for copy in copies:
        copy.start()
    expand = spread()
    eye = iota((TL, TL), 0) == iota((TL, TL), 1)
    for copy in copies:
        copy.wait()
    weights = jnp.where(eye, counts[...].astype(F32), 0.0).astype(BF)
    good = flags[...].astype(F32).astype(BF)
    terms_ref[...] = dot(weights, good).astype(BF)
    for k in range(2 * NB // SW):
        masks_ref[:, k * SW : (k + 1) * SW] = dot(good[:, k * SW // 2 : (k + 1) * SW // 2], expand).astype(BF)


def weigh(flags, counts):
    return pl.pallas_call(
        weigh_kernel,
        in_specs=[pl.BlockSpec(memory_space=pl.ANY)] * 2,
        out_shape=[jax.ShapeDtypeStruct((TL, NB), BF), jax.ShapeDtypeStruct((TL, 2 * NB), BF)],
        scratch_shapes=[
            pltpu.VMEM((TL, NB), jnp.int32),
            pltpu.VMEM((1, TL), jnp.int32),
            pltpu.SemaphoreType.DMA((2,)),
        ],
        compiler_params=limit(8),
        name="weigh",
    )(stay(flags), stay(counts))


def pack_kernel(vis_hbm, masks_ref, out_hbm, vis, blocks, sems, out_sems):
    copies = [pltpu.make_async_copy(vis_hbm.at[c], vis.at[c], sems.at[c]) for c in range(ND)]
    for copy in copies:
        copy.start()
    outs = []
    for c in range(ND):
        copies[c].wait()
        for j in range(NJ):
            cols = slice(j * JW, (j + 1) * JW)
            blocks[c * NJ + j] = vis[c, :, cols] * masks_ref[:, cols]
        part = pl.ds(c * NJ, NJ)
        outs.append(pltpu.make_async_copy(blocks.at[part], out_hbm.at[part], out_sems.at[c]))
        outs[-1].start()
    for copy in outs:
        copy.wait()


def pack(vis, masks):
    return pl.pallas_call(
        pack_kernel,
        in_specs=[pl.BlockSpec(memory_space=pl.ANY), pl.BlockSpec(memory_space=pltpu.VMEM)],
        out_specs=pl.BlockSpec(memory_space=pl.ANY),
        out_shape=jax.ShapeDtypeStruct((ND * NJ, TL, JW), BF),
        scratch_shapes=[
            pltpu.VMEM((ND, TL, 2 * NB), BF),
            pltpu.VMEM((ND * NJ, TL, JW), BF),
            pltpu.SemaphoreType.DMA((ND,)),
            pltpu.SemaphoreType.DMA((ND,)),
        ],
        compiler_params=limit(8),
        cost_estimate=pl.CostEstimate(flops=10**9, bytes_accessed=2 * 10**6, transcendentals=0),
        name="pack",
    )(stay(vis), masks)


def total_kernel(a_ref, b_ref, c_ref, d_ref, *out_refs):
    total = a_ref[...].astype(F32) + b_ref[...].astype(F32) + (c_ref[...].astype(F32) + d_ref[...].astype(F32))
    y = lax.axis_index("y")
    for k in range(NY):
        block = (y + k) % NY
        out = jnp.zeros((TL, BW), F32)
        for j in range(NY):
            out = jnp.where(block == j, total[:, j * BW : (j + 1) * BW], out)
        out_refs[k][...] = out.astype(BF)


def total(terms):
    return pl.pallas_call(
        total_kernel,
        out_shape=[jax.ShapeDtypeStruct((TL, BW), BF)] * NY,
        compiler_params=limit(4),
        name="total",
    )(*terms)


def average_kernel(got_ref, own_ref, one_ref, two_ref, three_ref, out_ref, dens):
    expand = spread()
    here = lax.axis_index("y")
    for k, ref in enumerate((own_ref, one_ref, two_ref, three_ref)):
        dens[(here - k + NY) % NY] = ref[...].astype(F32)
    values, turned = [], []
    for y in range(NY):
        num = got_ref[y].astype(F32)
        for d in range(1, ND):
            num += got_ref[d * NY + y].astype(F32)
        den = jnp.maximum(dens[y], 1.0).astype(BF)
        den = jnp.concatenate([dot(den[:, k : k + SW // 2], expand) for k in range(0, BW, SW // 2)], axis=1)
        averaged = (num / den).astype(BF)
        values.append(averaged.astype(F32))
        turned.append(turn(averaged) if y % 2 == 1 else None)
    even, odd = values[0] + values[2], values[1] + values[3]
    less, rest = values[0] - values[2], turned[1] - turned[3]
    sums = [even + odd, less + rest, even - odd, less - rest]
    for r in range(4):
        out_ref[r * TL : (r + 1) * TL, :] = sums[r].astype(BF)


def average(got, dens):
    return pl.pallas_call(
        average_kernel,
        out_shape=jax.ShapeDtypeStruct((4 * TL, JW), BF),
        scratch_shapes=[pltpu.VMEM((NY, TL, BW), F32)],
        compiler_params=limit(8),
        name="average",
    )(got, *dens)


def half_kernel(sums_ref, table_ref, out_ref):
    for r in range(4):
        x = sums_ref[r * TL : (r + 1) * TL, :]
        data = jnp.concatenate([x, turn(x).astype(BF)], axis=0)
        out_ref[r * QM : (r + 1) * QM, :] = dot(table_ref[r * QM : (r + 1) * QM, 0 : 2 * TL], data)


def half(sums, table):
    return pl.pallas_call(
        half_kernel,
        out_shape=jax.ShapeDtypeStruct((NM, JW), F32),
        compiler_params=limit(8),
        cost_estimate=pl.CostEstimate(flops=10**9, bytes_accessed=10**7, transcendentals=0),
        name="half",
    )(sums, table)


def transform_kernel(sums_ref, table_ref, half_ref, cols_ref, out_ref):
    parts = []
    for r in range(4):
        x = sums_ref[r * TL : (r + 1) * TL, :]
        data = jnp.concatenate([x, turn(x).astype(BF)], axis=0)
        parts.append(dot(table_ref[r * QM : (r + 1) * QM, 2 * TL : 4 * TL], data))
    part = jnp.concatenate(parts, axis=0) + half_ref[...]
    part = (part * (1.0 / math.sqrt(NT))).astype(BF)
    one_hot = jnp.where(cols_ref[...] == iota((NP * OS, NM), 1), 1.0, 0.0).astype(BF)
    rows = dot(one_hot, part)
    eight, groups = NP * 8, JW // NK
    first = [rows[0:eight, g * NK : (g + 1) * NK] for g in range(groups)]
    rest = [rows[eight:, g * NK : (g + 1) * NK] for g in range(groups)]
    rest = jnp.concatenate(rest, axis=0).astype(BF)
    line = iota((eight, groups * 2 * NP), 0)
    place, device = line % 8, line // 8
    source = place // 2 * (2 * NP) + 2 * device + place % 2
    last = dot(jnp.where(source == iota((eight, groups * 2 * NP), 1), 1.0, 0.0).astype(BF), rest)
    whole = jnp.concatenate([b.reshape(NP, 8, NK) for b in first + [last]], axis=1)
    out_ref[...] = whole.reshape(NP * PR, NK).astype(BF)


def transform(sums, table, own, cols):
    return pl.pallas_call(
        transform_kernel,
        out_shape=jax.ShapeDtypeStruct((NP * PR, NK), BF),
        compiler_params=limit(8),
        cost_estimate=pl.CostEstimate(flops=HIDE, bytes_accessed=HIDE // 300, transcendentals=0),
        name="transform",
    )(sums, table, own, cols)


def project_kernel(parts_ref, proj, weight_ref, basis, out_ref, mvis, turned, packed):
    for y in range(NY):
        total = parts_ref[y].astype(F32)
        for z in range(1, NZ):
            total += parts_ref[z * NY + y].astype(F32)
        for g in range(JW // NK):
            cols = slice(y * JW + g * NK, y * JW + (g + 1) * NK)
            mvis[0:8, cols] = total[8 * g : 8 * g + 8]
            last = total[32 + 2 * g : 34 + 2 * g]
            mvis[8:16, cols] = jnp.concatenate([last, jnp.zeros((6, NK), F32)], axis=0)
    left = mvis[...].astype(BF)
    slot = iota((SP, NK), 0)
    raw = jnp.zeros((SP, NK), F32)
    for s in range(OS):
        raw = jnp.where(slot == s, dot(left, proj[s]), raw)
    coef = (raw * weight_ref[...]).astype(BF)
    mode, row = iota((NK, 2 * NK), 0), iota((NK, 2 * NK), 1)
    left = [dot(coef, jnp.where(row == 2 * mode + q, 1.0, 0.0).astype(BF)) for q in range(2)]
    left = jnp.concatenate(left, axis=0).astype(BF)
    slot = iota((2 * SP, NR), 0) % SP
    profile = jnp.zeros((2 * SP, NR), F32)
    for s in range(OS):
        profile = jnp.where(slot == s, dot(left, basis[s].reshape(2 * NK, NR)), profile)
    turned[...] = profile.T
    pieces = [turned[pl.ds(r, SKY, stride=OR), :] for r in range(OR)]
    lines = EW // 128
    for i in range(lines):
        packed[pl.ds(i, SKY, stride=lines), :] = jnp.concatenate(pieces[4 * i : 4 * i + 4], axis=1)
    out_ref[...] = packed[...].astype(BF)


def project(parts, projection, weight, basis):
    return pl.pallas_call(
        project_kernel,
        out_shape=jax.ShapeDtypeStruct((SKY * EW // 128, 128), BF),
        scratch_shapes=[
            pltpu.VMEM((SP, 2 * NB), F32),
            pltpu.VMEM((NR, 2 * SP), F32),
            pltpu.VMEM((SKY * EW // 128, 128), F32),
        ],
        compiler_params=limit(8),
        name="project",
    )(parts, projection, weight, basis)


def nt(a, b):
    return lax.dot_general(a, b, (((1,), (1,)), ((), ())), preferred_element_type=F32)


def synthesis_kernel(got_ref, order_ref, table, out_ref, turned):
    got = got_ref[...].astype(F32)
    for i in range(EW // 128):
        turned[i * 128 : (i + 1) * 128, :] = got[:, i, :].T
    one_hot = jnp.where(iota((4 * QW, NM), 0) == order_ref[...], 1.0, 0.0).astype(BF)
    natural = []
    for q in range(2):
        pieces = [turned[pl.ds(q * SP + s, OR, stride=2 * SP), :] for s in range(OS)]
        slots = jnp.concatenate(pieces, axis=1).astype(BF)
        natural.append(nt(slots, one_hot).astype(BF))
    same, turn = [], []
    for r in range(4):
        real = natural[0][:, r * QW : r * QW + QM]
        imag = natural[1][:, r * QW : r * QW + QM]
        if r % 2 == 1:
            real, imag = jnp.concatenate([real, -imag], axis=0), jnp.concatenate([imag, real], axis=0)
        rows = 2 * r * QM
        both = dot(real, table[rows : rows + QM, :]) + dot(imag, table[rows + QM : rows + 2 * QM, :])
        same.append(both[0:OR])
        turn.append(both[OR:])
    quarters = [
        same[0] + same[2] + (same[1] + same[3]),
        same[0] - same[2] + (turn[1] - turn[3]),
        same[0] + same[2] - (same[1] + same[3]),
        same[0] - same[2] - (turn[1] - turn[3]),
    ]
    for k in range(4):
        out_ref[:, k * NPHI // 4 : (k + 1) * NPHI // 4] = quarters[k] * (1.0 / math.sqrt(NM))


def synthesis(got, order, table):
    vmem = pl.BlockSpec(memory_space=pltpu.VMEM)
    return pl.pallas_call(
        synthesis_kernel,
        out_shape=jax.ShapeDtypeStruct((OR, NPHI), F32),
        scratch_shapes=[
            pltpu.VMEM((EW, SKY), F32),
        ],
        compiler_params=limit(8),
        name="synthesis",
    )(got, order, table)


def body(visibility, flags, counts, m_order, projection, singular, cycles_basis):
    sky = ("y", "z", "core")
    terms, masks = weigh(flags[0], counts)
    days = [terms]
    for k in range(1, ND):
        days.append(lax.ppermute(terms, "day", [(i, (i + k) % ND) for i in range(ND)]))
    sent = pack(visibility[0], masks)
    got = lax.all_to_all(sent, ("day", "y"), split_axis=0, concat_axis=0, tiled=True)
    slots = m_order.reshape(SKY, OS)
    lines = slots % 4 * QM + slots // 4
    core = lax.axis_index("core")
    lines = lax.dynamic_index_in_dim(lines.reshape(NY, NZ, NC, OS), core, 2, keepdims=False)
    lines = lines.transpose(1, 0, 2).reshape(NP, OS)
    cols = jnp.concatenate([lines[:, 0:8].reshape(-1, 1), lines[:, 8:].reshape(-1, 1)], axis=0)
    places = slots % 4 * QW + slots // 4
    places = places.T.reshape(1, NM)
    table = lax.dynamic_index_in_dim(transform_table(), lax.axis_index("z") * NC + core, 0, keepdims=False)
    own = lax.dynamic_slice_in_dim(m_order, lax.axis_index(sky) * OS, OS)
    rank = NK - NK * own // (2 * NM)
    keep = jnp.arange(NK, dtype=jnp.int32)[None, :] < rank[:, None]
    sing = singular[0]
    weight = jnp.where(keep, sing / (sing * sing + 0.25), 0.0)
    weight = jnp.pad(weight, ((0, SP - OS), (0, 0)))
    got, table, cols, places, weight = lax.optimization_barrier((got, table, cols, places, weight))
    dens = list(total(days))
    for k in range(1, NY):
        dens[k] = lax.ppermute(dens[k], "y", [(i, (i + k) % NY) for i in range(NY)])
    sums = average(got, dens)
    others = lax.ppermute(sums, "core", [(0, 1), (1, 0)])
    packed = transform(others, table, half(sums, table), cols).reshape(NP, PR, NK)
    parts = lax.all_to_all(packed, ("z", "y"), split_axis=0, concat_axis=0, tiled=True)
    blocks = project(parts, projection[0], weight, cycles_basis[0]).reshape(SKY, EW // 128, 128)
    gathered = lax.all_to_all(blocks, sky, split_axis=0, concat_axis=0, tiled=True)
    return synthesis(gathered, places, jnp.asarray(synthesis_table()))[None]


def solution(mesh):
    fine = Mesh(mesh.devices.reshape(ND, NY, NZ, NC), ("day", "y", "z", "core"))
    sky = ("y", "z", "core")
    return jax.shard_map(
        body,
        mesh=fine,
        in_specs=(
            P("day", None, sky, None),
            P("day", sky, None),
            P("day", sky),
            P(),
            P("day", sky, None, None),
            P("day", sky, None),
            P("day", sky, None, None, None),
        ),
        out_specs=P("day", sky, None),
        check_vma=False,
    )
```

```python
import math

import jax
import jax.numpy as jnp
import ml_dtypes
import numpy as np
from jax import lax
from jax.experimental import pallas as pl
from jax.experimental.pallas import tpu as pltpu
from jax.sharding import Mesh
from jax.sharding import PartitionSpec as P

NB, NT, NM, NK, NR, NPHI = 1024, 4096, 640, 128, 1024, 2048
ND, NY, NZ, NC = 4, 4, 8, 2
SKY = NY * NZ * NC
NJ = NY
JW = 2 * NB // NJ
BW = NB // NJ
SW = 256
TL = NT // SKY
OS = NM // SKY
OR = NR // SKY
NP = NY * NZ
PR = 40
QM = NM // 4
QW = 256
SP = 16
EW = 2 * SP * OR
MIB = 1024 * 1024
HIDE = 3 * 10**9
BF, F32 = jnp.bfloat16, jnp.float32


def transform_table():
    m = np.arange(NM).reshape(QM, 4).T.reshape(1, NM, 1)
    z, c, other, t = np.ix_(np.arange(NZ), np.arange(NC), np.arange(2), np.arange(TL))
    times = ((z * NC + (c + other) % NC) * TL + t).reshape(NZ * NC, 1, 2, TL)
    angle = (m[..., None] * times % NT) * (2.0 * math.pi / NT)
    table = np.stack([np.cos(angle), np.sin(angle)], axis=3)
    return table.reshape(NZ * NC, NM, 4 * TL).astype(ml_dtypes.bfloat16)


def synthesis_table():
    p = np.arange(NPHI // 4)[None, :]
    out = np.zeros((4, 2, QM, NPHI // 4))
    for r in range(4):
        angle = (np.arange(r, NM, 4)[:, None] * p % NPHI) * (2.0 * math.pi / NPHI)
        out[r, 0], out[r, 1] = np.cos(angle), -np.sin(angle)
    return out.reshape(8 * QM, NPHI // 4).astype(ml_dtypes.bfloat16)


def iota(shape, dim):
    return lax.broadcasted_iota(jnp.int32, shape, dim)


def spread():
    return jnp.where(iota((SW // 2, SW), 0) == iota((SW // 2, SW), 1) // 2, 1.0, 0.0).astype(BF)


def turn(x):
    row, col = iota((SW, SW), 0), iota((SW, SW), 1)
    swap = jnp.where(row == col + 1, jnp.where(col % 2 == 0, 1.0, 0.0), 0.0)
    swap = swap - jnp.where(col == row + 1, jnp.where(col % 2 == 1, 1.0, 0.0), 0.0)
    swap = swap.astype(BF)
    return jnp.concatenate([dot(x[:, k : k + SW], swap) for k in range(0, JW, SW)], axis=1)


def dot(a, b):
    return jnp.dot(a, b, preferred_element_type=F32)


def limit(mib):
    return pltpu.CompilerParams(vmem_limit_bytes=mib * MIB)


def stay(x):
    return pltpu.with_memory_space_constraint(x, pltpu.HBM)


def weigh_kernel(flags_hbm, counts_hbm, vis_hbm, terms_ref, masks_ref, vis_ref, flags, counts, sems):
    copies = [
        pltpu.make_async_copy(flags_hbm, flags, sems.at[0]),
        pltpu.make_async_copy(counts_hbm, counts, sems.at[1]),
        pltpu.make_async_copy(vis_hbm, vis_ref, sems.at[2]),
    ]
    for copy in copies:
        copy.start()
    expand = spread()
    eye = iota((TL, TL), 0) == iota((TL, TL), 1)
    copies[0].wait()
    copies[1].wait()
    weights = jnp.where(eye, counts[...].astype(F32), 0.0).astype(BF)
    good = flags[...].astype(F32).astype(BF)
    terms_ref[...] = dot(weights, good).astype(BF)
    for k in range(2 * NB // SW):
        masks_ref[:, k * SW : (k + 1) * SW] = dot(good[:, k * SW // 2 : (k + 1) * SW // 2], expand).astype(BF)
    copies[2].wait()


def weigh(flags, counts, vis):
    vmem = pl.BlockSpec(memory_space=pltpu.VMEM)
    return pl.pallas_call(
        weigh_kernel,
        in_specs=[pl.BlockSpec(memory_space=pl.ANY)] * 3,
        out_specs=[vmem, vmem, pl.BlockSpec(memory_space=pl.ANY)],
        out_shape=[
            jax.ShapeDtypeStruct((TL, NB), BF),
            jax.ShapeDtypeStruct((TL, 2 * NB), BF),
            pltpu.VMEM((ND, TL, 2 * NB), BF),
        ],
        scratch_shapes=[
            pltpu.VMEM((TL, NB), jnp.int32),
            pltpu.VMEM((1, TL), jnp.int32),
            pltpu.SemaphoreType.DMA((3,)),
        ],
        compiler_params=limit(8),
        name="weigh",
    )(stay(flags), stay(counts), stay(vis))


def pack_kernel(vis_ref, masks_ref, out_hbm, blocks, out_sems):
    outs = []
    for c in range(ND):
        for j in range(NJ):
            cols = slice(j * JW, (j + 1) * JW)
            blocks[c * NJ + j] = vis_ref[c, :, cols] * masks_ref[:, cols]
        part = pl.ds(c * NJ, NJ)
        outs.append(pltpu.make_async_copy(blocks.at[part], out_hbm.at[part], out_sems.at[c]))
        outs[-1].start()
    for copy in outs:
        copy.wait()


def pack(vis, masks):
    return pl.pallas_call(
        pack_kernel,
        out_specs=pl.BlockSpec(memory_space=pl.ANY),
        out_shape=jax.ShapeDtypeStruct((ND * NJ, TL, JW), BF),
        scratch_shapes=[pltpu.VMEM((ND * NJ, TL, JW), BF), pltpu.SemaphoreType.DMA((ND,))],
        compiler_params=limit(8),
        cost_estimate=pl.CostEstimate(flops=10**9, bytes_accessed=2 * 10**6, transcendentals=0),
        name="pack",
    )(vis, masks)


def total_kernel(a_ref, b_ref, c_ref, d_ref, *out_refs):
    total = a_ref[...].astype(F32) + b_ref[...].astype(F32) + (c_ref[...].astype(F32) + d_ref[...].astype(F32))
    y = lax.axis_index("y")
    for k in range(NY):
        block = (y + k) % NY
        out = jnp.zeros((TL, BW), F32)
        for j in range(NY):
            out = jnp.where(block == j, total[:, j * BW : (j + 1) * BW], out)
        out_refs[k][...] = out.astype(BF)


def total(terms):
    return pl.pallas_call(
        total_kernel,
        out_shape=[jax.ShapeDtypeStruct((TL, BW), BF)] * NY,
        compiler_params=limit(4),
        name="total",
    )(*terms)


def average_kernel(got_ref, own_ref, one_ref, two_ref, three_ref, out_ref, dens):
    expand = spread()
    here = lax.axis_index("y")
    for k, ref in enumerate((own_ref, one_ref, two_ref, three_ref)):
        dens[(here - k + NY) % NY] = ref[...].astype(F32)
    values, turned = [], []
    for y in range(NY):
        num = got_ref[y].astype(F32)
        for d in range(1, ND):
            num += got_ref[d * NY + y].astype(F32)
        den = jnp.maximum(dens[y], 1.0).astype(BF)
        den = jnp.concatenate([dot(den[:, k : k + SW // 2], expand) for k in range(0, BW, SW // 2)], axis=1)
        averaged = (num / den).astype(BF)
        values.append(averaged.astype(F32))
        turned.append(turn(averaged) if y % 2 == 1 else None)
    even, odd = values[0] + values[2], values[1] + values[3]
    less, rest = values[0] - values[2], turned[1] - turned[3]
    sums = [even + odd, less + rest, even - odd, less - rest]
    for r in range(4):
        out_ref[r * TL : (r + 1) * TL, :] = sums[r].astype(BF)


def average(got, dens):
    return pl.pallas_call(
        average_kernel,
        out_shape=jax.ShapeDtypeStruct((4 * TL, JW), BF),
        scratch_shapes=[pltpu.VMEM((NY, TL, BW), F32)],
        compiler_params=limit(8),
        name="average",
    )(got, *dens)


def half_kernel(sums_ref, table_ref, out_ref):
    for r in range(4):
        x = sums_ref[r * TL : (r + 1) * TL, :]
        data = jnp.concatenate([x, turn(x).astype(BF)], axis=0)
        out_ref[r * QM : (r + 1) * QM, :] = dot(table_ref[r * QM : (r + 1) * QM, 0 : 2 * TL], data)


def half(sums, table):
    return pl.pallas_call(
        half_kernel,
        out_shape=jax.ShapeDtypeStruct((NM, JW), F32),
        compiler_params=limit(8),
        cost_estimate=pl.CostEstimate(flops=10**9, bytes_accessed=10**7, transcendentals=0),
        name="half",
    )(sums, table)


def transform_kernel(sums_ref, table_ref, half_ref, cols_ref, out_ref):
    parts = []
    for r in range(4):
        x = sums_ref[r * TL : (r + 1) * TL, :]
        data = jnp.concatenate([x, turn(x).astype(BF)], axis=0)
        parts.append(dot(table_ref[r * QM : (r + 1) * QM, 2 * TL : 4 * TL], data))
    part = jnp.concatenate(parts, axis=0) + half_ref[...]
    part = (part * (1.0 / math.sqrt(NT))).astype(BF)
    one_hot = jnp.where(cols_ref[...] == iota((NP * OS, NM), 1), 1.0, 0.0).astype(BF)
    rows = dot(one_hot, part)
    eight, groups = NP * 8, JW // NK
    first = [rows[0:eight, g * NK : (g + 1) * NK] for g in range(groups)]
    rest = [rows[eight:, g * NK : (g + 1) * NK] for g in range(groups)]
    rest = jnp.concatenate(rest, axis=0).astype(BF)
    line = iota((eight, groups * 2 * NP), 0)
    place, device = line % 8, line // 8
    source = place // 2 * (2 * NP) + 2 * device + place % 2
    last = dot(jnp.where(source == iota((eight, groups * 2 * NP), 1), 1.0, 0.0).astype(BF), rest)
    whole = jnp.concatenate([b.reshape(NP, 8, NK) for b in first + [last]], axis=1)
    out_ref[...] = whole.reshape(NP * PR, NK).astype(BF)


def transform(sums, table, own, cols):
    return pl.pallas_call(
        transform_kernel,
        out_shape=jax.ShapeDtypeStruct((NP * PR, NK), BF),
        compiler_params=limit(8),
        cost_estimate=pl.CostEstimate(flops=HIDE, bytes_accessed=HIDE // 300, transcendentals=0),
        name="transform",
    )(sums, table, own, cols)


def project_kernel(parts_ref, proj, weight_ref, basis, out_ref, mvis, turned, packed):
    for y in range(NY):
        total = parts_ref[y].astype(F32)
        for z in range(1, NZ):
            total += parts_ref[z * NY + y].astype(F32)
        for g in range(JW // NK):
            cols = slice(y * JW + g * NK, y * JW + (g + 1) * NK)
            mvis[0:8, cols] = total[8 * g : 8 * g + 8]
            last = total[32 + 2 * g : 34 + 2 * g]
            mvis[8:16, cols] = jnp.concatenate([last, jnp.zeros((6, NK), F32)], axis=0)
    left = mvis[...].astype(BF)
    slot = iota((SP, NK), 0)
    raw = jnp.zeros((SP, NK), F32)
    for s in range(OS):
        raw = jnp.where(slot == s, dot(left, proj[s]), raw)
    coef = (raw * weight_ref[...]).astype(BF)
    mode, row = iota((NK, 2 * NK), 0), iota((NK, 2 * NK), 1)
    left = [dot(coef, jnp.where(row == 2 * mode + q, 1.0, 0.0).astype(BF)) for q in range(2)]
    left = jnp.concatenate(left, axis=0).astype(BF)
    slot = iota((2 * SP, NR), 0) % SP
    profile = jnp.zeros((2 * SP, NR), F32)
    for s in range(OS):
        profile = jnp.where(slot == s, dot(left, basis[s].reshape(2 * NK, NR)), profile)
    turned[...] = profile.T
    pieces = [turned[pl.ds(r, SKY, stride=OR), :] for r in range(OR)]
    lines = EW // 128
    for i in range(lines):
        packed[pl.ds(i, SKY, stride=lines), :] = jnp.concatenate(pieces[4 * i : 4 * i + 4], axis=1)
    out_ref[...] = packed[...].astype(BF)


def project(parts, projection, weight, basis):
    return pl.pallas_call(
        project_kernel,
        out_shape=jax.ShapeDtypeStruct((SKY * EW // 128, 128), BF),
        scratch_shapes=[
            pltpu.VMEM((SP, 2 * NB), F32),
            pltpu.VMEM((NR, 2 * SP), F32),
            pltpu.VMEM((SKY * EW // 128, 128), F32),
        ],
        compiler_params=limit(8),
        name="project",
    )(parts, projection, weight, basis)


def nt(a, b):
    return lax.dot_general(a, b, (((1,), (1,)), ((), ())), preferred_element_type=F32)


def synthesis_kernel(got_ref, order_ref, table, out_ref, turned):
    got = got_ref[...].astype(F32)
    for i in range(EW // 128):
        turned[i * 128 : (i + 1) * 128, :] = got[:, i, :].T
    one_hot = jnp.where(iota((4 * QW, NM), 0) == order_ref[...], 1.0, 0.0).astype(BF)
    natural = []
    for q in range(2):
        pieces = [turned[pl.ds(q * SP + s, OR, stride=2 * SP), :] for s in range(OS)]
        slots = jnp.concatenate(pieces, axis=1).astype(BF)
        natural.append(nt(slots, one_hot).astype(BF))
    same, turn = [], []
    for r in range(4):
        real = natural[0][:, r * QW : r * QW + QM]
        imag = natural[1][:, r * QW : r * QW + QM]
        if r % 2 == 1:
            real, imag = jnp.concatenate([real, -imag], axis=0), jnp.concatenate([imag, real], axis=0)
        rows = 2 * r * QM
        both = dot(real, table[rows : rows + QM, :]) + dot(imag, table[rows + QM : rows + 2 * QM, :])
        same.append(both[0:OR])
        turn.append(both[OR:])
    quarters = [
        same[0] + same[2] + (same[1] + same[3]),
        same[0] - same[2] + (turn[1] - turn[3]),
        same[0] + same[2] - (same[1] + same[3]),
        same[0] - same[2] - (turn[1] - turn[3]),
    ]
    for k in range(4):
        out_ref[:, k * NPHI // 4 : (k + 1) * NPHI // 4] = quarters[k] * (1.0 / math.sqrt(NM))


def synthesis(got, order, table):
    vmem = pl.BlockSpec(memory_space=pltpu.VMEM)
    return pl.pallas_call(
        synthesis_kernel,
        out_shape=jax.ShapeDtypeStruct((OR, NPHI), F32),
        scratch_shapes=[
            pltpu.VMEM((EW, SKY), F32),
        ],
        compiler_params=limit(8),
        name="synthesis",
    )(got, order, table)


def body(visibility, flags, counts, m_order, projection, singular, cycles_basis):
    sky = ("y", "z", "core")
    terms, masks, held = weigh(flags[0], counts, visibility[0])
    days = [terms]
    for k in range(1, ND):
        days.append(lax.ppermute(terms, "day", [(i, (i + k) % ND) for i in range(ND)]))
    sent = pack(held, masks)
    got = lax.all_to_all(sent, ("day", "y"), split_axis=0, concat_axis=0, tiled=True)
    slots = m_order.reshape(SKY, OS)
    lines = slots % 4 * QM + slots // 4
    core = lax.axis_index("core")
    lines = lax.dynamic_index_in_dim(lines.reshape(NY, NZ, NC, OS), core, 2, keepdims=False)
    lines = lines.transpose(1, 0, 2).reshape(NP, OS)
    cols = jnp.concatenate([lines[:, 0:8].reshape(-1, 1), lines[:, 8:].reshape(-1, 1)], axis=0)
    places = slots % 4 * QW + slots // 4
    places = places.T.reshape(1, NM)
    table = lax.dynamic_index_in_dim(transform_table(), lax.axis_index("z") * NC + core, 0, keepdims=False)
    own = lax.dynamic_slice_in_dim(m_order, lax.axis_index(sky) * OS, OS)
    rank = NK - NK * own // (2 * NM)
    keep = jnp.arange(NK, dtype=jnp.int32)[None, :] < rank[:, None]
    sing = singular[0]
    weight = jnp.where(keep, sing / (sing * sing + 0.25), 0.0)
    weight = jnp.pad(weight, ((0, SP - OS), (0, 0)))
    got, table, cols, places, weight = lax.optimization_barrier((got, table, cols, places, weight))
    dens = list(total(days))
    for k in range(1, NY):
        dens[k] = lax.ppermute(dens[k], "y", [(i, (i + k) % NY) for i in range(NY)])
    sums = average(got, dens)
    others = lax.ppermute(sums, "core", [(0, 1), (1, 0)])
    packed = transform(others, table, half(sums, table), cols).reshape(NP, PR, NK)
    parts = lax.all_to_all(packed, ("z", "y"), split_axis=0, concat_axis=0, tiled=True)
    blocks = project(parts, projection[0], weight, cycles_basis[0]).reshape(SKY, EW // 128, 128)
    gathered = lax.all_to_all(blocks, sky, split_axis=0, concat_axis=0, tiled=True)
    return synthesis(gathered, places, jnp.asarray(synthesis_table()))[None]


def solution(mesh):
    fine = Mesh(mesh.devices.reshape(ND, NY, NZ, NC), ("day", "y", "z", "core"))
    sky = ("y", "z", "core")
    return jax.shard_map(
        body,
        mesh=fine,
        in_specs=(
            P("day", None, sky, None),
            P("day", sky, None),
            P("day", sky),
            P(),
            P("day", sky, None, None),
            P("day", sky, None),
            P("day", sky, None, None, None),
        ),
        out_specs=P("day", sky, None),
        check_vma=False,
    )
```

```python
import math

import jax
import jax.numpy as jnp
import ml_dtypes
import numpy as np
from jax import lax
from jax.experimental import pallas as pl
from jax.experimental.pallas import tpu as pltpu
from jax.sharding import Mesh
from jax.sharding import PartitionSpec as P

NB, NT, NM, NK, NR, NPHI = 1024, 4096, 640, 128, 1024, 2048
ND, NY, NZ, NC = 4, 4, 8, 2
SKY = NY * NZ * NC
NJ = NY
JW = 2 * NB // NJ
BW = NB // NJ
SW = 256
TL = NT // SKY
OS = NM // SKY
OR = NR // SKY
NP = NY * NZ
PR = 40
QM = NM // 4
QW = 256
SP = 16
EW = 2 * SP * OR
MIB = 1024 * 1024
HIDE = 3 * 10**9
BF, F32 = jnp.bfloat16, jnp.float32


def transform_table():
    m = np.arange(NM).reshape(QM, 4).T.reshape(1, NM, 1)
    z, c, other, t = np.ix_(np.arange(NZ), np.arange(NC), np.arange(2), np.arange(TL))
    times = ((z * NC + (c + other) % NC) * TL + t).reshape(NZ * NC, 1, 2, TL)
    angle = (m[..., None] * times % NT) * (2.0 * math.pi / NT)
    table = np.stack([np.cos(angle), np.sin(angle)], axis=3)
    return table.reshape(NZ * NC, NM, 4 * TL).astype(ml_dtypes.bfloat16)


def synthesis_table():
    p = np.arange(NPHI // 4)[None, :]
    out = np.zeros((4, 2, QM, NPHI // 4))
    for r in range(4):
        angle = (np.arange(r, NM, 4)[:, None] * p % NPHI) * (2.0 * math.pi / NPHI)
        out[r, 0], out[r, 1] = np.cos(angle), -np.sin(angle)
    return out.reshape(8 * QM, NPHI // 4).astype(ml_dtypes.bfloat16)


def iota(shape, dim):
    return lax.broadcasted_iota(jnp.int32, shape, dim)


def spread():
    return jnp.where(iota((SW // 2, SW), 0) == iota((SW // 2, SW), 1) // 2, 1.0, 0.0).astype(BF)


def turn(x):
    row, col = iota((SW, SW), 0), iota((SW, SW), 1)
    swap = jnp.where(row == col + 1, jnp.where(col % 2 == 0, 1.0, 0.0), 0.0)
    swap = swap - jnp.where(col == row + 1, jnp.where(col % 2 == 1, 1.0, 0.0), 0.0)
    swap = swap.astype(BF)
    return jnp.concatenate([dot(x[:, k : k + SW], swap) for k in range(0, JW, SW)], axis=1)


def dot(a, b):
    return jnp.dot(a, b, preferred_element_type=F32)


def limit(mib):
    return pltpu.CompilerParams(vmem_limit_bytes=mib * MIB)


def stay(x):
    return pltpu.with_memory_space_constraint(x, pltpu.HBM)


def weigh_kernel(flags_hbm, counts_hbm, vis_hbm, terms_ref, masks_ref, vis_ref, flags, counts, sems):
    copies = [
        pltpu.make_async_copy(flags_hbm, flags, sems.at[0]),
        pltpu.make_async_copy(counts_hbm, counts, sems.at[1]),
        pltpu.make_async_copy(vis_hbm, vis_ref, sems.at[2]),
    ]
    for copy in copies:
        copy.start()
    expand = spread()
    eye = iota((TL, TL), 0) == iota((TL, TL), 1)
    copies[0].wait()
    copies[1].wait()
    weights = jnp.where(eye, counts[...].astype(F32), 0.0).astype(BF)
    good = flags[...].astype(F32).astype(BF)
    terms_ref[...] = dot(weights, good).astype(BF)
    for k in range(2 * NB // SW):
        masks_ref[:, k * SW : (k + 1) * SW] = dot(good[:, k * SW // 2 : (k + 1) * SW // 2], expand).astype(BF)
    copies[2].wait()


def weigh(flags, counts, vis):
    vmem = pl.BlockSpec(memory_space=pltpu.VMEM)
    return pl.pallas_call(
        weigh_kernel,
        in_specs=[pl.BlockSpec(memory_space=pl.ANY)] * 3,
        out_specs=[vmem, vmem, pl.BlockSpec(memory_space=pl.ANY)],
        out_shape=[
            jax.ShapeDtypeStruct((TL, NB), BF),
            jax.ShapeDtypeStruct((TL, 2 * NB), BF),
            pltpu.VMEM((ND, TL, 2 * NB), BF),
        ],
        scratch_shapes=[
            pltpu.VMEM((TL, NB), jnp.int32),
            pltpu.VMEM((1, TL), jnp.int32),
            pltpu.SemaphoreType.DMA((3,)),
        ],
        compiler_params=limit(8),
        name="weigh",
    )(stay(flags), stay(counts), stay(vis))


def pack_kernel(vis_ref, masks_ref, out_hbm, blocks, out_sems):
    outs = []
    for c in range(ND):
        for j in range(NJ):
            cols = slice(j * JW, (j + 1) * JW)
            blocks[c * NJ + j] = vis_ref[c, :, cols] * masks_ref[:, cols]
        part = pl.ds(c * NJ, NJ)
        outs.append(pltpu.make_async_copy(blocks.at[part], out_hbm.at[part], out_sems.at[c]))
        outs[-1].start()
    for copy in outs:
        copy.wait()


def pack(vis, masks):
    return pl.pallas_call(
        pack_kernel,
        out_specs=pl.BlockSpec(memory_space=pl.ANY),
        out_shape=jax.ShapeDtypeStruct((ND * NJ, TL, JW), BF),
        scratch_shapes=[pltpu.VMEM((ND * NJ, TL, JW), BF), pltpu.SemaphoreType.DMA((ND,))],
        compiler_params=limit(8),
        cost_estimate=pl.CostEstimate(flops=10**9, bytes_accessed=2 * 10**6, transcendentals=0),
        name="pack",
    )(vis, masks)


def total_kernel(a_ref, b_ref, c_ref, d_ref, *out_refs):
    total = a_ref[...].astype(F32) + b_ref[...].astype(F32) + (c_ref[...].astype(F32) + d_ref[...].astype(F32))
    y = lax.axis_index("y")
    for k in range(NY):
        block = (y + k) % NY
        out = jnp.zeros((TL, BW), F32)
        for j in range(NY):
            out = jnp.where(block == j, total[:, j * BW : (j + 1) * BW], out)
        out_refs[k][...] = out.astype(BF)


def total(terms):
    return pl.pallas_call(
        total_kernel,
        out_shape=[jax.ShapeDtypeStruct((TL, BW), BF)] * NY,
        compiler_params=limit(4),
        name="total",
    )(*terms)


def average_kernel(got_ref, own_ref, one_ref, two_ref, three_ref, out_ref, dens):
    expand = spread()
    here = lax.axis_index("y")
    for k, ref in enumerate((own_ref, one_ref, two_ref, three_ref)):
        dens[(here - k + NY) % NY] = ref[...].astype(F32)
    values, turned = [], []
    for y in range(NY):
        num = got_ref[y].astype(F32)
        for d in range(1, ND):
            num += got_ref[d * NY + y].astype(F32)
        den = jnp.maximum(dens[y], 1.0).astype(BF)
        den = jnp.concatenate([dot(den[:, k : k + SW // 2], expand) for k in range(0, BW, SW // 2)], axis=1)
        averaged = (num / den).astype(BF)
        values.append(averaged.astype(F32))
        turned.append(turn(averaged) if y % 2 == 1 else None)
    even, odd = values[0] + values[2], values[1] + values[3]
    less, rest = values[0] - values[2], turned[1] - turned[3]
    sums = [even + odd, less + rest, even - odd, less - rest]
    for r in range(4):
        out_ref[r * TL : (r + 1) * TL, :] = sums[r].astype(BF)


def average(got, dens):
    return pl.pallas_call(
        average_kernel,
        out_shape=jax.ShapeDtypeStruct((4 * TL, JW), BF),
        scratch_shapes=[pltpu.VMEM((NY, TL, BW), F32)],
        compiler_params=limit(8),
        name="average",
    )(got, *dens)


def half_kernel(sums_ref, table_ref, out_ref):
    for r in range(4):
        x = sums_ref[r * TL : (r + 1) * TL, :]
        data = jnp.concatenate([x, turn(x).astype(BF)], axis=0)
        out_ref[r * QM : (r + 1) * QM, :] = dot(table_ref[r * QM : (r + 1) * QM, 0 : 2 * TL], data)


def half(sums, table):
    return pl.pallas_call(
        half_kernel,
        out_shape=jax.ShapeDtypeStruct((NM, JW), F32),
        compiler_params=limit(8),
        cost_estimate=pl.CostEstimate(flops=10**9, bytes_accessed=10**7, transcendentals=0),
        name="half",
    )(sums, table)


def transform_kernel(sums_ref, table_ref, half_ref, cols_ref, out_ref):
    parts = []
    for r in range(4):
        x = sums_ref[r * TL : (r + 1) * TL, :]
        data = jnp.concatenate([x, turn(x).astype(BF)], axis=0)
        parts.append(dot(table_ref[r * QM : (r + 1) * QM, 2 * TL : 4 * TL], data))
    part = jnp.concatenate(parts, axis=0) + half_ref[...]
    part = (part * (1.0 / math.sqrt(NT))).astype(BF)
    one_hot = jnp.where(cols_ref[...] == iota((NP * OS, NM), 1), 1.0, 0.0).astype(BF)
    rows = dot(one_hot, part)
    eight, groups = NP * 8, JW // NK
    first = [rows[0:eight, g * NK : (g + 1) * NK] for g in range(groups)]
    rest = [rows[eight:, g * NK : (g + 1) * NK] for g in range(groups)]
    rest = jnp.concatenate(rest, axis=0).astype(BF)
    line = iota((eight, groups * 2 * NP), 0)
    place, device = line % 8, line // 8
    source = place // 2 * (2 * NP) + 2 * device + place % 2
    last = dot(jnp.where(source == iota((eight, groups * 2 * NP), 1), 1.0, 0.0).astype(BF), rest)
    whole = jnp.concatenate([b.reshape(NP, 8, NK) for b in first + [last]], axis=1)
    out_ref[...] = whole.reshape(NP * PR, NK).astype(BF)


def transform(sums, table, own, cols):
    return pl.pallas_call(
        transform_kernel,
        out_shape=jax.ShapeDtypeStruct((NP * PR, NK), BF),
        compiler_params=limit(8),
        cost_estimate=pl.CostEstimate(flops=HIDE, bytes_accessed=HIDE // 300, transcendentals=0),
        name="transform",
    )(sums, table, own, cols)


def project_kernel(parts_ref, proj, weight_ref, basis, out_ref, mvis, turned, packed):
    for y in range(NY):
        total = parts_ref[y].astype(F32)
        for z in range(1, NZ):
            total += parts_ref[z * NY + y].astype(F32)
        for g in range(JW // NK):
            cols = slice(y * JW + g * NK, y * JW + (g + 1) * NK)
            mvis[0:8, cols] = total[8 * g : 8 * g + 8]
            last = total[32 + 2 * g : 34 + 2 * g]
            mvis[8:16, cols] = jnp.concatenate([last, jnp.zeros((6, NK), F32)], axis=0)
    left = mvis[...].astype(BF)
    slot = iota((SP, 2 * NB), 0)
    none = jnp.zeros((SP, 2 * NB), BF)
    wide = jnp.concatenate([jnp.where(slot == s, left, none) for s in range(OS)], axis=1)
    raw = dot(wide, proj[...].reshape(OS * 2 * NB, NK))
    coef = (raw * weight_ref[...]).astype(BF)
    mode, row = iota((NK, 2 * NK), 0), iota((NK, 2 * NK), 1)
    left = [dot(coef, jnp.where(row == 2 * mode + q, 1.0, 0.0).astype(BF)) for q in range(2)]
    left = jnp.concatenate(left, axis=0).astype(BF)
    slot = iota((2 * SP, 2 * NK), 0) % SP
    none = jnp.zeros((2 * SP, 2 * NK), BF)
    wide = jnp.concatenate([jnp.where(slot == s, left, none) for s in range(OS)], axis=1)
    profile = dot(wide, basis[...].reshape(OS * 2 * NK, NR))
    turned[...] = profile.T
    pieces = [turned[pl.ds(r, SKY, stride=OR), :] for r in range(OR)]
    lines = EW // 128
    for i in range(lines):
        packed[pl.ds(i, SKY, stride=lines), :] = jnp.concatenate(pieces[4 * i : 4 * i + 4], axis=1)
    out_ref[...] = packed[...].astype(BF)


def project(parts, projection, weight, basis):
    return pl.pallas_call(
        project_kernel,
        out_shape=jax.ShapeDtypeStruct((SKY * EW // 128, 128), BF),
        scratch_shapes=[
            pltpu.VMEM((SP, 2 * NB), F32),
            pltpu.VMEM((NR, 2 * SP), F32),
            pltpu.VMEM((SKY * EW // 128, 128), F32),
        ],
        compiler_params=limit(8),
        name="project",
    )(parts, projection, weight, basis)


def nt(a, b):
    return lax.dot_general(a, b, (((1,), (1,)), ((), ())), preferred_element_type=F32)


def synthesis_kernel(got_ref, order_ref, table, out_ref, turned):
    got = got_ref[...].astype(F32)
    for i in range(EW // 128):
        turned[i * 128 : (i + 1) * 128, :] = got[:, i, :].T
    one_hot = jnp.where(iota((4 * QW, NM), 0) == order_ref[...], 1.0, 0.0).astype(BF)
    natural = []
    for q in range(2):
        pieces = [turned[pl.ds(q * SP + s, OR, stride=2 * SP), :] for s in range(OS)]
        slots = jnp.concatenate(pieces, axis=1).astype(BF)
        natural.append(nt(slots, one_hot).astype(BF))
    same, turn = [], []
    for r in range(4):
        real = natural[0][:, r * QW : r * QW + QM]
        imag = natural[1][:, r * QW : r * QW + QM]
        if r % 2 == 1:
            real, imag = jnp.concatenate([real, -imag], axis=0), jnp.concatenate([imag, real], axis=0)
        rows = 2 * r * QM
        both = dot(real, table[rows : rows + QM, :]) + dot(imag, table[rows + QM : rows + 2 * QM, :])
        same.append(both[0:OR])
        turn.append(both[OR:])
    quarters = [
        same[0] + same[2] + (same[1] + same[3]),
        same[0] - same[2] + (turn[1] - turn[3]),
        same[0] + same[2] - (same[1] + same[3]),
        same[0] - same[2] - (turn[1] - turn[3]),
    ]
    for k in range(4):
        out_ref[:, k * NPHI // 4 : (k + 1) * NPHI // 4] = quarters[k] * (1.0 / math.sqrt(NM))


def synthesis(got, order, table):
    vmem = pl.BlockSpec(memory_space=pltpu.VMEM)
    return pl.pallas_call(
        synthesis_kernel,
        out_shape=jax.ShapeDtypeStruct((OR, NPHI), F32),
        scratch_shapes=[
            pltpu.VMEM((EW, SKY), F32),
        ],
        compiler_params=limit(8),
        name="synthesis",
    )(got, order, table)


def body(visibility, flags, counts, m_order, projection, singular, cycles_basis):
    sky = ("y", "z", "core")
    terms, masks, held = weigh(flags[0], counts, visibility[0])
    days = [terms]
    for k in range(1, ND):
        days.append(lax.ppermute(terms, "day", [(i, (i + k) % ND) for i in range(ND)]))
    sent = pack(held, masks)
    got = lax.all_to_all(sent, ("day", "y"), split_axis=0, concat_axis=0, tiled=True)
    slots = m_order.reshape(SKY, OS)
    lines = slots % 4 * QM + slots // 4
    core = lax.axis_index("core")
    lines = lax.dynamic_index_in_dim(lines.reshape(NY, NZ, NC, OS), core, 2, keepdims=False)
    lines = lines.transpose(1, 0, 2).reshape(NP, OS)
    cols = jnp.concatenate([lines[:, 0:8].reshape(-1, 1), lines[:, 8:].reshape(-1, 1)], axis=0)
    places = slots % 4 * QW + slots // 4
    places = places.T.reshape(1, NM)
    table = lax.dynamic_index_in_dim(transform_table(), lax.axis_index("z") * NC + core, 0, keepdims=False)
    own = lax.dynamic_slice_in_dim(m_order, lax.axis_index(sky) * OS, OS)
    rank = NK - NK * own // (2 * NM)
    keep = jnp.arange(NK, dtype=jnp.int32)[None, :] < rank[:, None]
    sing = singular[0]
    weight = jnp.where(keep, sing / (sing * sing + 0.25), 0.0)
    weight = jnp.pad(weight, ((0, SP - OS), (0, 0)))
    got, table, cols, places, weight = lax.optimization_barrier((got, table, cols, places, weight))
    dens = list(total(days))
    for k in range(1, NY):
        dens[k] = lax.ppermute(dens[k], "y", [(i, (i + k) % NY) for i in range(NY)])
    sums = average(got, dens)
    others = lax.ppermute(sums, "core", [(0, 1), (1, 0)])
    packed = transform(others, table, half(sums, table), cols).reshape(NP, PR, NK)
    parts = lax.all_to_all(packed, ("z", "y"), split_axis=0, concat_axis=0, tiled=True)
    blocks = project(parts, projection[0], weight, cycles_basis[0]).reshape(SKY, EW // 128, 128)
    gathered = lax.all_to_all(blocks, sky, split_axis=0, concat_axis=0, tiled=True)
    return synthesis(gathered, places, jnp.asarray(synthesis_table()))[None]


def solution(mesh):
    fine = Mesh(mesh.devices.reshape(ND, NY, NZ, NC), ("day", "y", "z", "core"))
    sky = ("y", "z", "core")
    return jax.shard_map(
        body,
        mesh=fine,
        in_specs=(
            P("day", None, sky, None),
            P("day", sky, None),
            P("day", sky),
            P(),
            P("day", sky, None, None),
            P("day", sky, None),
            P("day", sky, None, None, None),
        ),
        out_specs=P("day", sky, None),
        check_vma=False,
    )
```
